512 devices in a mesh: row: 32 (over y, x), layer: 16 (over z, core).
Axes of the slice: x: 4, y: 8, z: 8, core: 2. Of those that a mesh axis runs over, the one named last changes fastest.
Arguments:
- panel_left: bfloat16 [32, 32, 2048, 128], P('row', 'layer'), may hold values from -6 to 6
- panel_right: bfloat16 [32, 32, 2048, 128], P('row', 'layer'), may hold values from -0.125 to 0.125
- test_matrix: bfloat16 [2048, 128], replicated, may hold values from -6 to 6
- ranks: int32 [32, 32], P('row', 'layer'), may hold values from 32 to 128, as said below
- offsets: int32 [32, 2], P('row'), may hold values from 1 to 4, as said below
Outputs:
- basis: float32 [32, 2048, 2, 128], P('row', 'layer')
- update_right: float32 [32, 2048, 2, 128], P('row', 'layer')
The draws below stay inside these ranges and needn't reach their ends.
Inputs may be any that keep to these rules, and one draw needn't show every extreme that they name: `ranks`: some tile has rank 128 and some tile has rank 128 // 4. An owner's 2 offsets differ from each other; the values 1 and 4 occur in every draw.
All inputs are finite; a program needn't handle non-finite values.
Results may differ from the reference program's by a relative error of at most 0.0003.
Values may be sent and summed in bfloat16 or wider, within the bound.
A program may use at most 64 MiB of HBM per device.

```python
import jax
import jax.numpy as jnp
from jax import lax

B = 2048
R = 128
FRONTS = 4
TARGETS = 2
OWNERS = 32
LAYERS = 32


def draw_ranks(key, part):
    draws_all = jax.random.randint(key, (OWNERS, LAYERS), R // 4, R + 1, dtype=jnp.int32)
    return draws_all.at[0, 0].set(R).at[0, 1].set(R // 4)


def draw_offsets(key, part):
    row_keys = jax.random.split(jax.random.fold_in(key, 7), OWNERS)
    orders = jax.vmap(lambda row_key: jax.random.permutation(row_key, FRONTS))(row_keys)
    picked = orders[:, :TARGETS].astype(jnp.int32) + 1
    return picked.at[0].set(jnp.array([1, FRONTS], dtype=jnp.int32))


def levels(key, dims, shards, smallest, high):
    gain, own = 1.0, jax.random.fold_in(key, 6)
    for position, blocks in shards:
        heights = jnp.exp(jax.random.uniform(jax.random.fold_in(own, position), (blocks,), jnp.float32, smallest / len(shards), high / len(shards)))
        gain = gain * jnp.repeat(heights, dims[position] // blocks).reshape([-1 if axis == position else 1 for axis in range(len(dims))])
    return gain


def centred(stream_key, extent, width, limit, shards=(), held_as=jnp.bfloat16):
    gain = levels(stream_key, extent, shards, -0.22, 0.18) if shards else 1.0
    values = jax.random.normal(stream_key, extent, jnp.float32) * width * gain
    return jnp.minimum(jnp.maximum(values, -limit), limit).astype(held_as)


def setup_inputs(seed: int = 0) -> dict:
    streams_of = jax.random.split(jax.random.key(seed), 6)
    return {
        "panel_left": centred(streams_of[0], (OWNERS, LAYERS, B, R), 1.0, 6.0, ((0, 32), (1, 16))),
        "panel_right": centred(streams_of[1], (OWNERS, LAYERS, B, R), B ** -0.5, 0.125, ((0, 32), (1, 16))),
        "test_matrix": centred(streams_of[2], (B, R), 1.0, 6.0),
        "ranks": draw_ranks(jax.random.fold_in(streams_of[5], 71), 0),
        "offsets": draw_offsets(jax.random.fold_in(streams_of[5], 71), 0),
    }


def orthonormal(sketch_rows, gram_mat):
    factor = jnp.linalg.cholesky(gram_mat)
    by_cols = jnp.transpose(sketch_rows, (1, 2, 0))
    solved = lax.linalg.triangular_solve(factor, by_cols, left_side=True, lower=True)
    return jnp.transpose(solved, (2, 0, 1))

def reference(panel_left, panel_right, test_matrix, ranks, offsets):
    columns = jnp.arange(R, dtype=jnp.int32)
    high = lax.Precision.HIGHEST
    test_full = test_matrix.astype(jnp.float32)

    def masked(owner_idx):
        live_cols = (columns[None, :] < ranks[owner_idx][:, None]).astype(jnp.bfloat16)
        own_left = lax.dynamic_index_in_dim(panel_left, owner_idx, 0, keepdims=False) * live_cols[:, None, :]
        own_right = lax.dynamic_index_in_dim(panel_right, owner_idx, 0, keepdims=False) * live_cols[:, None, :]
        return (own_left.astype(jnp.float32), own_right.astype(jnp.float32))

    def per_owner(owner_idx):
        own_left, own_right = masked(owner_idx)
        cores = []
        mixers = []
        partners = []
        for target in range(TARGETS):
            partner = ((owner_idx - offsets[owner_idx, target]) % OWNERS).astype(jnp.int32)
            other_left, other_right = masked(partner)
            core_mat = jnp.einsum('kbr,kbq->krq', own_right, other_right, precision=high)
            probes = jnp.einsum('kbr,bq->krq', other_left, test_full, precision=high)
            mix_mat = jnp.einsum('krq,kqs->krs', core_mat, probes, precision=high)
            cores.append(core_mat)
            mixers.append(mix_mat)
            partners.append(other_left)
        mixed = jnp.stack(mixers, axis=1)
        total_sketch = jnp.einsum('kbr,ksrq->bsq', own_left, mixed, precision=high)
        gram_mat = jnp.einsum('bsr,bsq->srq', total_sketch, total_sketch, precision=high) / B
        basis_part = orthonormal(total_sketch, gram_mat)
        reach = jnp.einsum('kbr,bsq->ksrq', own_left, basis_part, precision=high)
        term_list = []
        for target in range(TARGETS):
            weights = jnp.einsum('krq,krs->kqs', cores[target], reach[:, target], precision=high)
            term_list.append(jnp.einsum('kbq,kqs->bs', partners[target], weights, precision=high))
        update_part = jnp.stack(term_list, axis=1) / B
        return (basis_part, update_part)
    basis, update_right = lax.map(per_owner, jnp.arange(OWNERS, dtype=jnp.int32))
    return (basis, update_right)
```

```python
import functools

import jax
import jax.numpy as jnp
from jax import lax
from jax.experimental import pallas as pl
from jax.experimental.pallas import tpu as pltpu
from jax.sharding import PartitionSpec as P

R = 128
X = 4
FRONTS = 4
TARGETS = 2
BF = jnp.bfloat16
F32 = jnp.float32
HIGH = lax.Precision.HIGHEST


def dot(a, b, ca=1, cb=0, precision=None):
    return lax.dot_general(
        a, b, (((ca,), (cb,)), ((), ())), precision=precision, preferred_element_type=F32
    )


def split(a):
    high = a.astype(BF)
    return high, (a - high.astype(F32)).astype(BF)


def kernel(
    rows, layers, tile,
    u_ref, v_ref, test_ref, ranks_ref, offs_ref,
    basis_ref, upd_ref,
    un, um, vm, vq, uq, usel, meta, metas, probe_own, probes, parts, chain_in, plain_in, sum_out, sum_in, core,
    mix, s_part, s_cx, s_send, s_recv, s_own, s_full, gx, linv, reach, wall, t_part, t_cx, t_send, t_recv, t_own, t_fin,
    a2v_s, a2v_r, a2u_s, a2u_r, yv_s, yv_r, yu_s, yu_r, mt_s, mt_r, pr_s, pr_r, cr_s, cr_r,
    scx_s, scx_r, srs_s, srs_r, ag_s, ag_r, agc_s, agc_r, wg_s, wg_r, tcx_s, tcx_r, trs_s, trs_r, fin_s, fin_r,
):
    ny, nz = rows // X, layers // 2
    np_, nm = nz // 2, nz - 1 - nz // 2
    br = tile // layers
    qr, hb = br // X, br // 2
    quarter = tile // X
    row, layer = lax.axis_index("row"), lax.axis_index("layer")
    x, y = lax.rem(row, X), lax.div(row, X)
    z, c = lax.div(layer, 2), lax.rem(layer, 2)

    def xdev(d):
        return (y * X + lax.rem(x + d, X), layer)

    def ydev(d):
        return (lax.rem(y + d + ny, ny) * X + x, layer)

    def zdev(d):
        return (row, lax.rem(z + d + nz, nz) * 2 + c)

    mate = (row, z * 2 + 1 - c)
    barrier = pltpu.get_barrier_semaphore()
    friends = [xdev(1), xdev(2), xdev(3), ydev(1), ydev(-1), zdev(1), zdev(-1), mate]
    for friend in friends:
        pl.semaphore_signal(barrier, inc=1, device_id=friend, device_id_type=pl.DeviceIdType.MESH)

    def remote(src, dst, ssem, rsem, dev):
        return pltpu.make_async_remote_copy(
            src_ref=src, dst_ref=dst, send_sem=ssem, recv_sem=rsem,
            device_id=dev, device_id_type=pl.DeviceIdType.MESH,
        )

    pending = []

    def start(copy):
        copy.start()
        pending.append(copy)
        return copy

    lanes = lax.broadcasted_iota(jnp.int32, (1, R), 1)
    live = [(lanes < ranks_ref[0, k]).astype(F32).astype(BF) for k in range(2)]

    def mask_rows(i, carry):
        src = pl.ds(pl.multiple_of(i * br, br), br)
        for k in range(2):
            v = v_ref[0, k, src, :] * live[k]
            for xx in range(X):
                vm[xx, k, pl.ds(pl.multiple_of(i * qr, qr), qr), :] = v[xx * qr:(xx + 1) * qr]
        return carry

    lax.fori_loop(0, layers, mask_rows, 0)
    vq[X + x] = vm[x]
    for s in range(TARGETS):
        meta[s, :, :] = jnp.full((8, R), offs_ref[0, s], jnp.int32).astype(F32)
    metas[x] = meta[...]
    pl.semaphore_wait(barrier, len(friends))

    def slot_of(d):
        return lax.rem(x - d + X, X)

    def a2a(d, src, dst, ss, rs):
        return remote(src.at[lax.rem(x + d, X)], dst.at[X + x], ss.at[d], rs.at[d], xdev(d))

    def ysend(d, buf, ss, rs):
        return remote(buf.at[X + slot_of(d)], buf.at[slot_of(d)], ss.at[d], rs.at[d], ydev(1))

    yv = [ysend(d, vq, yv_s, yv_r) for d in range(X)]
    start(yv[0])
    av = {d: start(a2a(d, vm, vq, a2v_s, a2v_r)) for d in (2, 1, 3)}
    mts = {d: start(remote(meta, metas.at[x], mt_s.at[d], mt_r.at[d], xdev(d))) for d in (1, 2, 3)}

    def mask_left(i, carry):
        src = pl.ds(pl.multiple_of(i * br, br), br)
        for k in range(2):
            u = u_ref[0, k, src, :] * live[k]
            un[k, src, :] = u
            for xx in range(X):
                um[xx, k, pl.ds(pl.multiple_of(i * qr, qr), qr), :] = u[xx * qr:(xx + 1) * qr]
        return carry

    lax.fori_loop(0, layers, mask_left, 0)
    uq[X + x] = um[x]
    for k in range(2):
        probe_own[k] = jnp.zeros((R, R), F32)

    def probe_rows(i, carry):
        src = pl.ds(pl.multiple_of(i * br, br), br)
        for k in range(2):
            probe_own[k] += dot(un[k, src, :], test_ref[src, :], 0, 0)
        return carry

    lax.fori_loop(0, layers, probe_rows, 0)
    pry = start(remote(probe_own, probes.at[FRONTS - 1], pr_s.at[0], pr_r.at[0], ydev(1)))
    for d in (1, 3, 2):
        av[d].wait_recv()
        start(yv[d])

    def probe_send(d, src):
        return remote(src, probes.at[d - 1], pr_s.at[d], pr_r.at[d], xdev(d))

    for d in (1, 2, 3):
        @pl.when(x + d < X)
        def _(d=d):
            probe_send(d, probe_own).start()
    pry.wait_recv()
    for d in (1, 2, 3):
        @pl.when(x + d >= X)
        def _(d=d):
            probe_send(d, probes.at[FRONTS - 1]).start()
    prx = [probe_send(d, probe_own) for d in (1, 2, 3)]
    pending.extend(prx)
    for copy in mts.values():
        copy.wait_recv()
    for d in range(X):
        yv[d].wait_recv()

    yu = [ysend(d, uq, yu_s, yu_r) for d in range(X)]
    start(yu[0])

    picks = [[[(metas[xx, s, 0:1, :] == o).astype(F32) for o in range(1, FRONTS + 1)]
              for s in range(TARGETS)] for xx in range(X)]

    for xx in range(X):
        for k in range(2):
            mine = vq[X + xx, k]
            found = [dot(mine, vq[X + xx - o, k], 0, 0) for o in range(1, FRONTS + 1)]
            for s in range(TARGETS):
                total = found[0] * picks[xx][s][0]
                for o in range(1, FRONTS):
                    total = total + found[o] * picks[xx][s][o]
                parts[xx, s, k] = total

    far = lax.rem(x + 2, X)
    right, left = lax.rem(x + 1, X), lax.rem(x + 3, X)
    far0 = start(remote(parts.at[far, 0], chain_in.at[0], cr_s.at[0], cr_r.at[0], xdev(3)))
    far1 = start(remote(parts.at[far, 1], chain_in.at[1], cr_s.at[1], cr_r.at[1], xdev(1)))
    plain0 = start(remote(parts.at[right, 0], plain_in.at[0], cr_s.at[2], cr_r.at[2], xdev(1)))
    plain1 = start(remote(parts.at[left, 1], plain_in.at[1], cr_s.at[3], cr_r.at[3], xdev(3)))
    far0.wait_recv()
    sum_out[0] = parts[left, 0] + chain_in[0]
    sum0 = start(remote(sum_out.at[0], sum_in.at[0], cr_s.at[4], cr_r.at[4], xdev(3)))
    far1.wait_recv()
    sum_out[1] = parts[right, 1] + chain_in[1]
    sum1 = start(remote(sum_out.at[1], sum_in.at[1], cr_s.at[5], cr_r.at[5], xdev(1)))
    for copy in prx:
        copy.wait_recv()
    plain0.wait_recv()
    plain1.wait_recv()
    sum0.wait_recv()
    sum1.wait_recv()
    for s in range(TARGETS):
        core[s] = parts[x, s] + plain_in[s] + sum_in[s]

    au = {d: start(a2a(d, um, uq, a2u_s, a2u_r)) for d in (2, 1, 3)}

    for s in range(TARGETS):
        for k in range(2):
            back = jnp.clip(offs_ref[0, s] - 1, 0, FRONTS - 1)
            mixed = dot(core[s, k], probes[back, k], precision=HIGH)
            high, low = split(mixed)
            mix[0, k * R:(k + 1) * R, s * R:(s + 1) * R] = high
            mix[1, k * R:(k + 1) * R, s * R:(s + 1) * R] = low

    def order(i):
        half = lax.div(i + 1, 2)
        off = jnp.where(lax.rem(i, 2) == 1, half - np_, np_ - half)
        return lax.rem(z + off + nz, nz)

    def pair_copy(part, cx, ss, rs, zz):
        return remote(part.at[1 - c, zz], cx.at[zz], ss.at[zz], rs.at[zz], mate)

    def sketch_rows(i, carry):
        zz = order(i)
        for other in (1, 0):
            par = 1 - c if other else c
            src = pl.ds(pl.multiple_of((zz * 2 + par) * br, br), br)
            both = jnp.concatenate([un[0, src, :], un[1, src, :]], axis=1)
            s_part[par, zz] = dot(both, mix[0]) + dot(both, mix[1])
            if other:
                pair_copy(s_part, s_cx, scx_s, scx_r, zz).start()
        return carry

    lax.fori_loop(0, nz, sketch_rows, 0)

    chains = [(1, 0, np_), (-1, 0, nm), (1, 1, nm), (-1, 1, np_)]

    def ring_reduce(part, cx, send, recv, ss_cx, rs_cx, ss, rs, own, between):
        waited = set()

        def term(off, h):
            zz = lax.rem(z + off + 2 * nz, nz)
            if off % nz not in waited:
                waited.add(off % nz)
                pair_copy(part, cx, ss_cx, rs_cx, zz).wait_recv()
            at = pl.ds(h * hb, hb)
            return part[c, zz, at, :] + cx[zz, at, :]

        def hop(ch, i):
            return remote(send.at[ch, i], recv.at[ch, i], ss.at[ch, i], rs.at[ch, i], zdev(chains[ch][0]))

        for i in range(np_):
            for ch, (sgn, h, n) in enumerate(chains):
                j = i - (np_ - n)
                if j < 0:
                    continue
                value = term(sgn * (n - j), h)
                if j > 0:
                    hop(ch, j - 1).wait_recv()
                    value = value + recv[ch, j - 1]
                send[ch, j] = value
                start(hop(ch, j))
            between(i)
        for h in range(2):
            value = term(0, h)
            for ch, (sgn, hh, n) in enumerate(chains):
                if hh == h and n > 0:
                    hop(ch, n - 1).wait_recv()
                    value = value + recv[ch, n - 1]
            own[h * hb:(h + 1) * hb, :] = value

    def forward_left(i):
        for d in {0: (1,), 1: (3,), 2: (2,)}.get(i, ()):
            au[d].wait_recv()
            start(yu[d])

    if np_ >= 3:
        ring_reduce(s_part, s_cx, s_send, s_recv, scx_s, scx_r, srs_s, srs_r, s_own, forward_left)
    else:
        ring_reduce(s_part, s_cx, s_send, s_recv, scx_s, scx_r, srs_s, srs_r, s_own, lambda i: None)
        for i in range(3):
            forward_left(i)

    high, low = split(s_own[...])
    for h in range(2):
        s_full[c, z, h, 0] = high[h * hb:(h + 1) * hb]
        s_full[c, z, h, 1] = low[h * hb:(h + 1) * hb]

    def gather_hop(ch, i):
        sgn, h, n = chains[ch]
        zz = lax.rem(z - sgn * i + nz, nz)
        return remote(s_full.at[c, zz, h], s_full.at[c, zz, h], ag_s.at[ch, i], ag_r.at[ch, i], zdev(sgn))

    def to_mate(off, h):
        zz = lax.rem(z + off + nz, nz)
        at = (off + nz) % nz
        return remote(s_full.at[c, zz, h], s_full.at[c, zz, h], agc_s.at[at, h], agc_r.at[at, h], mate)

    for ch, (sgn, h, n) in enumerate(chains):
        if n > 0:
            start(gather_hop(ch, 0))
    for h in range(2):
        start(to_mate(0, h))
    for i in range(np_):
        for ch, (sgn, h, n) in enumerate(chains):
            if i < n:
                gather_hop(ch, i).wait_recv()
                if i + 1 < n:
                    start(gather_hop(ch, i + 1))
                start(to_mate(-sgn * (i + 1), h))
    for off in range(nz):
        for h in range(2):
            to_mate(off, h).wait_recv()

    reach[...] = jnp.zeros_like(reach)
    gx[...] = jnp.zeros_like(gx)

    def reach_rows(zz, carry):
        src = pl.ds(pl.multiple_of(zz * 2 * br, 2 * br), 2 * br)
        both = jnp.concatenate([un[0, src, :], un[1, src, :]], axis=1)
        pieces = [(a, b) for a in range(2) for b in range(2)]
        shigh = jnp.concatenate([s_full[a, zz, b, 0] for a, b in pieces], axis=0)
        slow = jnp.concatenate([s_full[a, zz, b, 1] for a, b in pieces], axis=0)
        reach[...] += dot(both, shigh, 0, 0) + dot(both, slow, 0, 0)
        for s in range(TARGETS):
            at = slice(s * R, (s + 1) * R)
            gx[s, :, 0:R] += dot(shigh[:, at], shigh[:, at], 0, 0)
            gx[s, :, R:2 * R] += dot(shigh[:, at], slow[:, at], 0, 0)
        return carry

    lax.fori_loop(0, nz, reach_rows, 0)

    for s in range(TARGETS):
        for k in range(2):
            weight = dot(core[s, k], reach[k * R:(k + 1) * R, s * R:(s + 1) * R], 0, 0, precision=HIGH)
            high, low = split(weight)
            wall[x, s, k * R:(k + 1) * R, 0:R] = high
            wall[x, s, k * R:(k + 1) * R, R:2 * R] = low

    def weight_send(i, who, s, d):
        return remote(wall.at[who, s], wall.at[who, s], wg_s.at[i], wg_r.at[i], xdev(d))

    wr1 = start(weight_send(0, x, 1, 1))
    wl0 = start(weight_send(1, x, 0, 3))
    wr0 = start(weight_send(2, x, 0, 1))
    wl1 = start(weight_send(3, x, 1, 3))

    eye = (lax.broadcasted_iota(jnp.int32, (R, R), 0) == lax.broadcasted_iota(jnp.int32, (R, R), 1)).astype(F32)
    for s in range(TARGETS):
        cross = gx[s, :, R:2 * R]
        gx[s, :, 0:R] = (gx[s, :, 0:R] + (cross + cross.T)) / tile
        gx[s, :, R:2 * R] = eye

    lane8 = lax.broadcasted_iota(jnp.int32, (8, R), 1)
    sub8 = lax.broadcasted_iota(jnp.int32, (8, R), 0)

    def factor_block(b, carry):
        r0 = pl.multiple_of(b * 8, 8)
        for s in range(TARGETS):
            gg = gx[s, pl.ds(r0, 8), 0:R]
            xx = gx[s, pl.ds(r0, 8), R:2 * R]
            cols = [
                jnp.broadcast_to(
                    jnp.sum(jnp.where(lane8 == r0 + j, gg, 0.0), axis=1, keepdims=True), (8, R))
                for j in range(8)
            ]
            diag = jnp.ones((8, R), F32)
            for j in range(8):
                pivot = cols[j][j:j + 1]
                diag = jnp.where(sub8 == j, pivot, diag)
                f = jnp.where(sub8 > j, cols[j] / pivot, 0.0)
                for m in range(j + 1, 8):
                    cols[m] = cols[m] - f * cols[m][j:j + 1]
                gg = gg - f * gg[j:j + 1]
                xx = xx - f * xx[j:j + 1]
            linv[s, pl.ds(r0, 8), :] = xx / jnp.sqrt(diag)
            lead = jnp.where(lane8 >= r0 + 8, gg / diag, 0.0)
            gx[s, :, 0:R] -= dot(lead, gg, 0, 0, precision=HIGH)
            gx[s, :, R:2 * R] -= dot(lead, xx, 0, 0, precision=HIGH)
        return carry

    blocks = R // 8
    lax.fori_loop(0, blocks // 4, factor_block, 0)
    wr1.wait_recv()
    fr1 = start(weight_send(4, left, 1, 1))
    wl0.wait_recv()
    fl0 = start(weight_send(5, right, 0, 3))

    for d in range(X):
        yu[d].wait_recv()
    pick16 = [[[w.astype(BF) for w in picks[xx][s]] for s in range(TARGETS)] for xx in range(X)]

    def choose_rows(i, carry):
        src = pl.ds(pl.multiple_of(i * 32, 32), 32)
        for xx in range(X):
            for k in range(2):
                cand = [uq[X + xx - o, k, src, :] for o in range(1, FRONTS + 1)]
                for s in range(TARGETS):
                    total = cand[0] * pick16[xx][s][0]
                    for o in range(1, FRONTS):
                        total = total + cand[o] * pick16[xx][s][o]
                    usel[xx, s, src, k * R:(k + 1) * R] = total
        return carry

    lax.fori_loop(0, quarter // 32, choose_rows, 0)
    lax.fori_loop(blocks // 4, blocks // 2, factor_block, 0)
    for copy in (wr0, wl1, fr1, fl0):
        copy.wait_recv()

    def term_rows(q, carry):
        src = pl.ds(pl.multiple_of(q * 4 * qr, 4 * qr), 4 * qr)
        for xx in range(X):
            for s in range(TARGETS):
                got = dot(usel[xx, s, src, :], wall[xx, s])
                got = got[:, 0:R] + got[:, R:2 * R]
                for i in range(4):
                    t_part[i % 2, q * 2 + i // 2, xx * qr:(xx + 1) * qr, s * R:(s + 1) * R] = got[i * qr:(i + 1) * qr]
        return carry

    lax.fori_loop(0, layers // 4, term_rows, 0)

    def pair_start(i, carry):
        pair_copy(t_part, t_cx, tcx_s, tcx_r, order(i)).start()
        return carry

    lax.fori_loop(0, nz, pair_start, 0)
    rest = blocks // 2

    def factor_more(i):
        lax.fori_loop(rest + i * rest // np_, rest + (i + 1) * rest // np_, factor_block, 0)

    ring_reduce(t_part, t_cx, t_send, t_recv, tcx_s, tcx_r, trs_s, trs_r, t_own, factor_more)

    def final_send(d):
        at = pl.ds(pl.multiple_of(lax.rem(x + d, X) * qr, qr), qr)
        return remote(t_own.at[at, :], t_fin.at[x], fin_s.at[d], fin_r.at[d], xdev(d))

    fins = [start(final_send(d)) for d in (2, 1, 3)]
    t_fin[x] = t_own[pl.ds(pl.multiple_of(x * qr, qr), qr), :]
    for s in range(TARGETS):
        at = slice(s * R, (s + 1) * R)
        basis_ref[0, :, s, :] = dot(s_own[:, at], linv[s], 1, 1, precision=HIGH)
    for copy in fins:
        copy.wait_recv()
    for s in range(TARGETS):
        at = slice(s * R, (s + 1) * R)
        terms = jnp.concatenate([t_fin[i, :, at] for i in range(X)], axis=0)
        upd_ref[0, :, s, :] = dot(terms, linv[s], 1, 1, precision=HIGH) / tile

    for copy in pending:
        copy.wait_send()

    def pair_end(zz, carry):
        pair_copy(s_part, s_cx, scx_s, scx_r, zz).wait_send()
        pair_copy(t_part, t_cx, tcx_s, tcx_r, zz).wait_send()
        return carry

    lax.fori_loop(0, nz, pair_end, 0)


def on_device(panel_left, panel_right, test_matrix, ranks, offsets):
    rows, layers = lax.axis_size("row"), lax.axis_size("layer")
    tile = panel_left.shape[2]
    nz = layers // 2
    np_ = max(nz // 2, 1)
    br = tile // layers
    qr, hb, quarter = br // X, br // 2, tile // X
    dma = pltpu.SemaphoreType.DMA
    vmem = pltpu.VMEM
    ring = [
        vmem((2, nz, br, 2 * R), F32), vmem((nz, br, 2 * R), F32),
        vmem((4, np_, hb, 2 * R), F32), vmem((4, np_, hb, 2 * R), F32), vmem((br, 2 * R), F32),
    ]
    scratch = [
        vmem((2, tile, R), BF), vmem((X, 2, quarter, R), BF), vmem((X, 2, quarter, R), BF),
        vmem((2 * X, 2, quarter, R), BF), vmem((2 * X, 2, quarter, R), BF),
        vmem((X, TARGETS, quarter, 2 * R), BF),
        vmem((TARGETS, 8, R), F32), vmem((X, TARGETS, 8, R), F32),
        vmem((2, R, R), F32), vmem((FRONTS, 2, R, R), F32),
        vmem((X, TARGETS, 2, R, R), F32),
        vmem((TARGETS, 2, R, R), F32), vmem((TARGETS, 2, R, R), F32), vmem((TARGETS, 2, R, R), F32),
        vmem((TARGETS, 2, R, R), F32), vmem((TARGETS, 2, R, R), F32),
        vmem((2, 2 * R, 2 * R), BF),
        *ring,
        vmem((2, nz, 2, 2, hb, 2 * R), BF),
        vmem((TARGETS, R, 2 * R), F32), vmem((TARGETS, R, R), F32), vmem((2 * R, 2 * R), F32),
        vmem((X, TARGETS, 2 * R, 2 * R), BF),
        *ring,
        vmem((X, qr, 2 * R), F32),
        dma((X,)), dma((X,)), dma((X,)), dma((X,)), dma((X,)), dma((X,)), dma((X,)), dma((X,)),
        dma((X,)), dma((X,)), dma((X,)), dma((X,)), dma((6,)), dma((6,)),
        dma((nz,)), dma((nz,)), dma((4, np_)), dma((4, np_)),
        dma((4, np_)), dma((4, np_)), dma((nz, 2)), dma((nz, 2)),
        dma((6,)), dma((6,)),
        dma((nz,)), dma((nz,)), dma((4, np_)), dma((4, np_)),
        dma((X,)), dma((X,)),
    ]
    inside = pl.BlockSpec(memory_space=pltpu.VMEM)
    scalars = pl.BlockSpec(memory_space=pltpu.SMEM)
    out = jax.ShapeDtypeStruct((1, br, TARGETS, R), F32)
    return pl.pallas_call(
        functools.partial(kernel, rows, layers, tile),
        out_shape=(out, out),
        in_specs=[inside, inside, inside, scalars, scalars],
        out_specs=(inside, inside),
        scratch_shapes=scratch,
        compiler_params=pltpu.CompilerParams(
            collective_id=0, has_side_effects=True, vmem_limit_bytes=50 * 2**20
        ),
        name="trailing_update",
    )(panel_left, panel_right, test_matrix, ranks, offsets)


def solution(mesh):
    return jax.shard_map(
        on_device,
        mesh=mesh,
        in_specs=(
            P("row", "layer", None, None),
            P("row", "layer", None, None),
            P(),
            P("row", "layer"),
            P("row", None),
        ),
        out_specs=(P("row", "layer", None, None), P("row", "layer", None, None)),
        check_vma=False,
    )
```

```python
import functools

import jax
import jax.numpy as jnp
from jax import lax
from jax.experimental import pallas as pl
from jax.experimental.pallas import tpu as pltpu
from jax.sharding import PartitionSpec as P

R = 128
X = 4
FRONTS = 4
TARGETS = 2
BF = jnp.bfloat16
F32 = jnp.float32
HIGH = lax.Precision.HIGHEST


def dot(a, b, ca=1, cb=0, precision=None):
    return lax.dot_general(
        a, b, (((ca,), (cb,)), ((), ())), precision=precision, preferred_element_type=F32
    )


def split(a):
    high = a.astype(BF)
    return high, (a - high.astype(F32)).astype(BF)


EXTRA = 16
STEPS = 128.0
TOP = 32766.0


def coded(value, ref, *at):
    n = value.shape[0]
    most = jnp.maximum(jnp.max(jnp.abs(value), axis=0, keepdims=True), 1e-30)
    code = jnp.ceil(jnp.log2(most) * STEPS) + 1.0
    ref[(*at, slice(0, n), slice(None))] = (
        jnp.round(value * (TOP * jnp.exp2(code * (-1.0 / STEPS)))).astype(jnp.int32).astype(jnp.int16)
    )
    ref[(*at, slice(n, n + EXTRA), slice(None))] = (
        jnp.broadcast_to(code, (EXTRA, value.shape[1])).astype(jnp.int32).astype(jnp.int16)
    )


def decoded(ref, *at):
    n = ref.shape[-2] - EXTRA
    code = ref[(*at, slice(n, n + EXTRA), slice(None))].astype(jnp.int32).astype(F32)[0:1]
    steps = ref[(*at, slice(0, n), slice(None))].astype(jnp.int32).astype(F32)
    return steps * (jnp.exp2(code * (1.0 / STEPS)) * (1.0 / TOP))


def kernel(
    rows, layers, tile,
    u_hbm, v_hbm, test_hbm, ranks_hbm, offs_hbm,
    basis_ref, upd_ref,
    u_ref, v_ref, test_ref, ranks_ref, offs_ref, in_sem, unt, vt, un, um, vm, vq, uq, usel, meta, metas, probe_own, probes, parts, far_out, plain_out, chain_in, plain_in, sum_out, sum_in, core,
    mix, s_part, s_out, s_cx, s_send, s_recv, s_own, s_all, s_full, gx, linv, reach, wall, w_all, t_part, t_out, t_cx, t_send, t_recv, t_own, t_fin,
    a2v_s, a2v_r, a2u_s, a2u_r, yv_s, yv_r, yu_s, yu_r, mt_s, mt_r, pr_s, pr_r, cr_s, cr_r,
    scx_s, scx_r, srs_s, srs_r, ag_s, ag_r, agc_s, agc_r, wg_s, wg_r, tcx_s, tcx_r, trs_s, trs_r, fin_s, fin_r,
):
    ny, nz = rows // X, layers // 2
    np_, nm = nz // 2, nz - 1 - nz // 2
    br = tile // layers
    qr, hb = br // X, br // 2
    quarter = tile // X
    row, layer = lax.axis_index("row"), lax.axis_index("layer")
    x, y = lax.rem(row, X), lax.div(row, X)
    z, c = lax.div(layer, 2), lax.rem(layer, 2)

    def xdev(d):
        return (y * X + lax.rem(x + d, X), layer)

    def ydev(d):
        return (lax.rem(y + d + ny, ny) * X + x, layer)

    def zdev(d):
        return (row, lax.rem(z + d + nz, nz) * 2 + c)

    mate = (row, z * 2 + 1 - c)
    loads = [
        pltpu.make_async_copy(src, dst, in_sem.at[i])
        for i, (src, dst) in enumerate((
            (ranks_hbm, ranks_ref), (offs_hbm, offs_ref), (v_hbm, v_ref), (u_hbm, u_ref), (test_hbm, test_ref)))
    ]
    for load in loads:
        load.start()
    barrier = pltpu.get_barrier_semaphore()
    friends = [xdev(1), xdev(2), xdev(3), ydev(1), ydev(-1), zdev(1), zdev(-1), mate]
    for friend in friends:
        pl.semaphore_signal(barrier, inc=1, device_id=friend, device_id_type=pl.DeviceIdType.MESH)

    def remote(src, dst, ssem, rsem, dev):
        return pltpu.make_async_remote_copy(
            src_ref=src, dst_ref=dst, send_sem=ssem, recv_sem=rsem,
            device_id=dev, device_id_type=pl.DeviceIdType.MESH,
        )

    pending = []

    def start(copy):
        copy.start()
        pending.append(copy)
        return copy

    loads[0].wait()
    loads[1].wait()
    lanes = lax.broadcasted_iota(jnp.int32, (1, R), 1)
    live = [(lanes < ranks_ref[0, k]).astype(F32).astype(BF) for k in range(2)]

    def mask_quarter(d):
        xx = lax.rem(x + d, X)

        def body(i, carry):
            src = pl.ds(pl.multiple_of(i * br + xx * qr, qr), qr)
            dst = pl.ds(pl.multiple_of(i * qr, qr), qr)
            for k in range(2):
                v = v_ref[0, k, src, :] * live[k]
                if d == 0:
                    vq[X + x, k, dst, :] = v
                else:
                    vm[xx, k, dst, :] = v
            return carry

        lax.fori_loop(0, layers, body, 0)

    def slot_of(d):
        return lax.rem(x - d + X, X)

    def a2a(d, src, dst, ss, rs):
        return remote(src.at[lax.rem(x + d, X)], dst.at[X + x], ss.at[d], rs.at[d], xdev(d))

    def ysend(d, buf, ss, rs):
        return remote(buf.at[X + slot_of(d)], buf.at[slot_of(d)], ss.at[d], rs.at[d], ydev(1))

    yv = [ysend(d, vq, yv_s, yv_r) for d in range(X)]
    av = [None] + [a2a(d, vm, vq, a2v_s, a2v_r) for d in (1, 2, 3)]
    loads[2].wait()
    mask_quarter(0)
    pl.semaphore_wait(barrier, len(friends))
    start(yv[0])
    mask_quarter(1)
    start(av[1])
    mask_quarter(3)
    start(av[3])
    mask_quarter(2)
    for s in range(TARGETS):
        meta[s, :, :] = jnp.full((8, R), offs_ref[0, s], jnp.int32).astype(F32)
    metas[x] = meta[...]
    mts = {d: start(remote(meta, metas.at[x], mt_s.at[d], mt_r.at[d], xdev(d))) for d in (1, 2, 3)}
    loads[3].wait()
    loads[4].wait()

    def mask_left(i, carry):
        src = pl.ds(pl.multiple_of(i * br, br), br)
        for k in range(2):
            u = u_ref[0, k, src, :] * live[k]
            un[k, src, :] = u
            unt[k * R:(k + 1) * R, src] = u.T
            for xx in range(X):
                um[xx, k, pl.ds(pl.multiple_of(i * qr, qr), qr), :] = u[xx * qr:(xx + 1) * qr]
        return carry

    lax.fori_loop(0, layers, mask_left, 0)
    uq[X + x] = um[x]
    probed = dot(unt[...], test_ref[...])
    for k in range(2):
        coded(probed[k * R:(k + 1) * R], probe_own, k)
    pry = start(remote(probe_own, probes.at[FRONTS - 1], pr_s.at[0], pr_r.at[0], ydev(1)))
    for d in (1, 3):
        av[d].wait_recv()
        start(yv[d])
    start(av[2])

    def probe_send(d, src):
        return remote(src, probes.at[d - 1], pr_s.at[d], pr_r.at[d], xdev(d))

    for d in (1, 2, 3):
        @pl.when(x + d < X)
        def _(d=d):
            probe_send(d, probe_own).start()
    for k in range(2):
        vt[k, pl.ds(pl.multiple_of(x * R, R), R), :] = vq[X + x, k].T
        for d in (1, 3):
            j = slot_of(d)
            vt[k, pl.ds(pl.multiple_of(j * R, R), R), :] = vq[X + j, k].T
    pry.wait_recv()
    for d in (1, 2, 3):
        @pl.when(x + d >= X)
        def _(d=d):
            probe_send(d, probes.at[FRONTS - 1]).start()
    prx = [probe_send(d, probe_own) for d in (1, 2, 3)]
    pending.extend(prx)
    av[2].wait_recv()
    start(yv[2])
    au = {d: a2a(d, um, uq, a2u_s, a2u_r) for d in (1, 2, 3)}
    start(au[1])
    start(au[3])
    for k in range(2):
        vt[k, pl.ds(pl.multiple_of(lax.rem(x + 2, X) * R, R), R), :] = vq[X + lax.rem(x + 2, X), k].T
    for copy in mts.values():
        copy.wait_recv()

    marks = [[metas[xx, s, 0:1, :] for s in range(TARGETS)] for xx in range(X)]
    parts[...] = jnp.zeros_like(parts)

    def add_cores(slot, first, back):
        for k in range(2):
            found = dot(vt[k, first * R:, :], vq[slot, k])
            for xx in range(first, X):
                block = found[(xx - first) * R:(xx - first + 1) * R]
                for s in range(TARGETS):
                    parts[xx, s, k] += block * (marks[xx][s] == back(xx)).astype(F32)

    for j in range(X - 1):
        add_cores(X + j, j + 1, lambda xx: float(xx - j))
    yu = [ysend(d, uq, yu_s, yu_r) for d in range(X)]
    for d in (0, 1, 3, 2):
        yv[d].wait_recv()
        j = slot_of(d)
        if d == 2:
            start(yu[0])
        add_cores(j, 0, lambda xx: (X + xx - j).astype(F32))

    far = lax.rem(x + 2, X)
    right, left = lax.rem(x + 1, X), lax.rem(x + 3, X)
    def code_part(who, s):
        for k in range(2):
            coded(parts[who, s, k], far_out if who is far else plain_out, s, k)

    code_part(far, 0)
    far0 = start(remote(far_out.at[0], chain_in.at[0], cr_s.at[0], cr_r.at[0], xdev(3)))
    code_part(far, 1)
    far1 = start(remote(far_out.at[1], chain_in.at[1], cr_s.at[1], cr_r.at[1], xdev(1)))
    code_part(right, 0)
    plain0 = start(remote(plain_out.at[0], plain_in.at[0], cr_s.at[2], cr_r.at[2], xdev(1)))
    code_part(left, 1)
    plain1 = start(remote(plain_out.at[1], plain_in.at[1], cr_s.at[3], cr_r.at[3], xdev(3)))
    far0.wait_recv()
    for k in range(2):
        coded(parts[left, 0, k] + decoded(chain_in, 0, k), sum_out, 0, k)
    sum0 = start(remote(sum_out.at[0], sum_in.at[0], cr_s.at[4], cr_r.at[4], xdev(3)))
    far1.wait_recv()
    for k in range(2):
        coded(parts[right, 1, k] + decoded(chain_in, 1, k), sum_out, 1, k)
    sum1 = start(remote(sum_out.at[1], sum_in.at[1], cr_s.at[5], cr_r.at[5], xdev(1)))
    for copy in prx:
        copy.wait_recv()
    plain0.wait_recv()
    plain1.wait_recv()
    sum0.wait_recv()
    sum1.wait_recv()
    for s in range(TARGETS):
        for k in range(2):
            core[s, k] = parts[x, s, k] + decoded(plain_in, s, k) + decoded(sum_in, s, k)

    start(au[2])
    for d in (1, 3):
        au[d].wait_recv()
        start(yu[d])

    for s in range(TARGETS):
        for k in range(2):
            back = jnp.clip(offs_ref[0, s] - 1, 0, FRONTS - 1)
            mixed = dot(core[s, k], decoded(probes, back, k), precision=HIGH)
            high, low = split(mixed)
            mix[0, k * R:(k + 1) * R, s * R:(s + 1) * R] = high
            mix[1, k * R:(k + 1) * R, s * R:(s + 1) * R] = low

    def order(i):
        half = lax.div(i + 1, 2)
        off = jnp.where(lax.rem(i, 2) == 1, half - np_, np_ - half)
        return lax.rem(z + off + nz, nz)

    def pair_copy(out, cx, ss, rs, zz):
        return remote(out.at[zz], cx.at[zz], ss.at[zz], rs.at[zz], mate)

    def sketch_rows(i, carry):
        zz = order(i)
        src = pl.ds(pl.multiple_of(zz * 2 * br, 2 * br), 2 * br)
        both = jnp.concatenate([un[0, src, :], un[1, src, :]], axis=1)
        got = dot(both, mix[0]) + dot(both, mix[1])
        s_part[0, zz] = got[:br]
        s_part[1, zz] = got[br:]
        for s in range(TARGETS):
            coded(s_part[1 - c, zz, :, s * R:(s + 1) * R], s_out, zz, s)
        pair_copy(s_out, s_cx, scx_s, scx_r, zz).start()
        return carry

    chains = [(1, 0, np_), (-1, 0, nm), (1, 1, nm), (-1, 1, np_)]

    def ring_reduce(part, out, cx, send, recv, ss_cx, rs_cx, ss, rs, own, before, between):
        waited = set()

        def term(off, h):
            zz = lax.rem(z + off + 2 * nz, nz)
            if off % nz not in waited:
                waited.add(off % nz)
                pair_copy(out, cx, ss_cx, rs_cx, zz).wait_recv()
            return part[c, zz, :, h * R:(h + 1) * R] + decoded(cx, zz, h)

        def hop(ch, i):
            return remote(send.at[ch, i], recv.at[ch, i], ss.at[ch, i], rs.at[ch, i], zdev(chains[ch][0]))

        for i in range(np_):
            before(i)
            for ch, (sgn, h, n) in enumerate(chains):
                j = i - (np_ - n)
                if j < 0:
                    continue
                value = term(sgn * (n - j), h)
                if j > 0:
                    hop(ch, j - 1).wait_recv()
                    value = value + decoded(recv, ch, j - 1)
                coded(value, send, ch, j)
                start(hop(ch, j))
            between(i)
        for h in range(2):
            value = term(0, h)
            for ch, (sgn, hh, n) in enumerate(chains):
                if hh == h and n > 0:
                    hop(ch, n - 1).wait_recv()
                    value = value + decoded(recv, ch, n - 1)
            own[:, h * R:(h + 1) * R] = value

    def sketch_more(i):
        lax.fori_loop(max(2 * i - 1, 0), nz if i == np_ - 1 else 2 * i + 1, sketch_rows, 0)

    ring_reduce(
        s_part, s_out, s_cx, s_send, s_recv, scx_s, scx_r, srs_s, srs_r, s_own, sketch_more, lambda i: None)
    au[2].wait_recv()
    start(yu[2])

    for h in range(2):
        coded(s_own[:, h * R:(h + 1) * R], s_all, c, z, h)

    def gather_hop(ch, i):
        sgn, h, n = chains[ch]
        zz = lax.rem(z - sgn * i + nz, nz)
        return remote(s_all.at[c, zz, h], s_all.at[c, zz, h], ag_s.at[ch, i], ag_r.at[ch, i], zdev(sgn))

    def to_mate(off, h):
        zz = lax.rem(z + off + nz, nz)
        at = (off + nz) % nz
        return remote(s_all.at[c, zz, h], s_all.at[c, zz, h], agc_s.at[at, h], agc_r.at[at, h], mate)

    def spread(par, off, h):
        zz = lax.rem(z + off + nz, nz)
        high, low = split(decoded(s_all, par, zz, h))
        to = pl.ds(pl.multiple_of((zz * 2 + par) * br, br), br)
        s_full[0, to, h * R:(h + 1) * R] = high
        s_full[1, to, h * R:(h + 1) * R] = low

    for ch, (sgn, h, n) in enumerate(chains):
        if n > 0:
            start(gather_hop(ch, 0))
    for h in range(2):
        start(to_mate(0, h))
    pick16 = [[[(marks[xx][s] == o).astype(F32).astype(BF) for o in range(1, FRONTS + 1)]
               for s in range(TARGETS)] for xx in range(X)]

    def choose_rows(i, carry):
        src = pl.ds(pl.multiple_of(i * 32, 32), 32)
        for xx in range(X):
            for k in range(2):
                cand = [uq[X + xx - o, k, src, :] for o in range(1, FRONTS + 1)]
                for s in range(TARGETS):
                    total = cand[0] * pick16[xx][s][0]
                    for o in range(1, FRONTS):
                        total = total + cand[o] * pick16[xx][s][o]
                    usel[xx, s, src, k * R:(k + 1) * R] = total
        return carry

    for h in range(2):
        spread(c, 0, h)
    late = [(0, h) for h in range(2)]
    for i in range(np_):
        got = []
        for ch, (sgn, h, n) in enumerate(chains):
            if i < n:
                gather_hop(ch, i).wait_recv()
                if i + 1 < n:
                    start(gather_hop(ch, i + 1))
                off = -sgn * (i + 1)
                start(to_mate(off, h))
                got.append((off, h))
        for off, h in late:
            to_mate(off, h).wait_recv()
            spread(1 - c, off, h)
        for off, h in got:
            spread(c, off, h)
        if i == min(1, np_ - 1):
            for d in range(X):
                yu[d].wait_recv()
            lax.fori_loop(0, quarter // 64, choose_rows, 0)
        if i == min(2, np_ - 1):
            lax.fori_loop(quarter // 64, quarter // 32, choose_rows, 0)
        late = got
    for off, h in late:
        to_mate(off, h).wait_recv()
        spread(1 - c, off, h)

    reach[...] = jnp.zeros_like(reach)
    gx[...] = jnp.zeros_like(gx)

    def reach_rows(zz, carry):
        src = pl.ds(pl.multiple_of(zz * 2 * br, 2 * br), 2 * br)
        reach[...] += dot(unt[:, src], s_full[0, src, :]) + dot(unt[:, src], s_full[1, src, :])
        return carry

    def gram_rows(zz, carry):
        src = pl.ds(pl.multiple_of(zz * 2 * br, 2 * br), 2 * br)
        for s in range(TARGETS):
            at = slice(s * R, (s + 1) * R)
            high, low = s_full[0, src, at], s_full[1, src, at]
            gx[s] += dot(high, jnp.concatenate([high, low], axis=1), 0, 0)
        return carry

    lax.fori_loop(0, nz, reach_rows, 0)

    for s in range(TARGETS):
        for k in range(2):
            weight = dot(core[s, k], reach[k * R:(k + 1) * R, s * R:(s + 1) * R], 0, 0, precision=HIGH)
            coded(weight, w_all, x, s, k)
            high, low = split(weight)
            wall[x, s, k * R:(k + 1) * R, 0:R] = high
            wall[x, s, k * R:(k + 1) * R, R:2 * R] = low

    def weight_send(i, who, s, d):
        return remote(w_all.at[who, s], w_all.at[who, s], wg_s.at[i], wg_r.at[i], xdev(d))

    wr1 = start(weight_send(0, x, 1, 1))
    wl0 = start(weight_send(1, x, 0, 3))
    wr0 = start(weight_send(2, x, 0, 1))
    wl1 = start(weight_send(3, x, 1, 3))

    lax.fori_loop(0, nz, gram_rows, 0)
    eye = (lax.broadcasted_iota(jnp.int32, (R, R), 0) == lax.broadcasted_iota(jnp.int32, (R, R), 1)).astype(F32)
    for s in range(TARGETS):
        cross = gx[s, :, R:2 * R]
        gx[s, :, 0:R] = (gx[s, :, 0:R] + (cross + cross.T)) / tile
        gx[s, :, R:2 * R] = eye

    lane8 = lax.broadcasted_iota(jnp.int32, (8, R), 1)
    sub8 = lax.broadcasted_iota(jnp.int32, (8, R), 0)

    def factor_block(b, carry):
        r0 = pl.multiple_of(b * 8, 8)
        for s in range(TARGETS):
            gg = gx[s, pl.ds(r0, 8), 0:R]
            xx = gx[s, pl.ds(r0, 8), R:2 * R]
            cols = [
                jnp.broadcast_to(
                    jnp.sum(jnp.where(lane8 == r0 + j, gg, 0.0), axis=1, keepdims=True), (8, R))
                for j in range(8)
            ]
            diag = jnp.ones((8, R), F32)
            for j in range(8):
                pivot = cols[j][j:j + 1]
                diag = jnp.where(sub8 == j, pivot, diag)
                f = jnp.where(sub8 > j, cols[j] / pivot, 0.0)
                for m in range(j + 1, 8):
                    cols[m] = cols[m] - f * cols[m][j:j + 1]
                gg = gg - f * gg[j:j + 1]
                xx = xx - f * xx[j:j + 1]
            linv[s, pl.ds(r0, 8), :] = xx / jnp.sqrt(diag)
            lead = jnp.where(lane8 >= r0 + 8, gg / diag, 0.0)
            gx[s, :, 0:R] -= dot(lead, gg, 0, 0, precision=HIGH)
            gx[s, :, R:2 * R] -= dot(lead, xx, 0, 0, precision=HIGH)
        return carry

    blocks = R // 8
    lax.fori_loop(0, blocks // 4, factor_block, 0)
    wr1.wait_recv()
    fr1 = start(weight_send(4, left, 1, 1))
    wl0.wait_recv()
    fl0 = start(weight_send(5, right, 0, 3))

    lax.fori_loop(blocks // 4, blocks // 2, factor_block, 0)
    for copy in (wr0, wl1, fr1, fl0):
        copy.wait_recv()
    for d in (1, 2, 3):
        who = lax.rem(x + d, X)
        for s in range(TARGETS):
            for k in range(2):
                high, low = split(decoded(w_all, who, s, k))
                wall[who, s, k * R:(k + 1) * R, 0:R] = high
                wall[who, s, k * R:(k + 1) * R, R:2 * R] = low

    span = layers // 2
    for q in range(2):
        src = slice(q * span * qr, (q + 1) * span * qr)
        for xx in range(X):
            for s in range(TARGETS):
                got = dot(usel[xx, s, src, :], wall[xx, s])
                got = got[:, 0:R] + got[:, R:2 * R]
                for i in range(span):
                    t_part[i % 2, (q * span + i) // 2, xx * qr:(xx + 1) * qr, s * R:(s + 1) * R] = got[i * qr:(i + 1) * qr]
        for zz in range(q * nz // 2, (q + 1) * nz // 2):
            for s in range(TARGETS):
                coded(t_part[1 - c, zz, :, s * R:(s + 1) * R], t_out, zz, s)
            pair_copy(t_out, t_cx, tcx_s, tcx_r, zz).start()
    rest = blocks // 2

    def factor_more(i):
        lax.fori_loop(rest + i * rest // np_, rest + (i + 1) * rest // np_, factor_block, 0)

    ring_reduce(t_part, t_out, t_cx, t_send, t_recv, tcx_s, tcx_r, trs_s, trs_r, t_own, lambda i: None, factor_more)

    def final_send(d):
        at = pl.ds(pl.multiple_of(lax.rem(x + d, X) * qr, qr), qr)
        return remote(t_own.at[at, :], t_fin.at[x], fin_s.at[d], fin_r.at[d], xdev(d))

    fins = [start(final_send(d)) for d in (2, 1, 3)]
    t_fin[x] = t_own[pl.ds(pl.multiple_of(x * qr, qr), qr), :]
    for s in range(TARGETS):
        at = slice(s * R, (s + 1) * R)
        basis_ref[0, :, s, :] = dot(s_own[:, at], linv[s], 1, 1, precision=HIGH)
    for copy in fins:
        copy.wait_recv()
    for s in range(TARGETS):
        at = slice(s * R, (s + 1) * R)
        terms = jnp.concatenate([t_fin[i, :, at] for i in range(X)], axis=0)
        upd_ref[0, :, s, :] = dot(terms, linv[s], 1, 1, precision=HIGH) / tile

    for copy in pending:
        copy.wait_send()

    def pair_end(zz, carry):
        pair_copy(s_out, s_cx, scx_s, scx_r, zz).wait_send()
        pair_copy(t_out, t_cx, tcx_s, tcx_r, zz).wait_send()
        return carry

    lax.fori_loop(0, nz, pair_end, 0)


def on_device(panel_left, panel_right, test_matrix, ranks, offsets):
    rows, layers = lax.axis_size("row"), lax.axis_size("layer")
    tile = panel_left.shape[2]
    nz = layers // 2
    np_ = max(nz // 2, 1)
    br = tile // layers
    qr, hb, quarter = br // X, br // 2, tile // X
    dma = pltpu.SemaphoreType.DMA
    vmem = pltpu.VMEM
    I16 = jnp.int16
    ring = [
        vmem((2, nz, br, 2 * R), F32), vmem((nz, 2, br + EXTRA, R), I16), vmem((nz, 2, br + EXTRA, R), I16),
        vmem((4, np_, br + EXTRA, R), I16), vmem((4, np_, br + EXTRA, R), I16), vmem((br, 2 * R), F32),
    ]
    scratch = [
        vmem((1, 2, tile, R), BF), vmem((1, 2, tile, R), BF), vmem((tile, R), BF),
        pltpu.SMEM((1, 2), jnp.int32), pltpu.SMEM((1, TARGETS), jnp.int32), dma((5,)),
        vmem((2 * R, tile), BF), vmem((2, X * R, quarter), BF),
        vmem((2, tile, R), BF), vmem((X, 2, quarter, R), BF), vmem((X, 2, quarter, R), BF),
        vmem((2 * X, 2, quarter, R), BF), vmem((2 * X, 2, quarter, R), BF),
        vmem((X, TARGETS, quarter, 2 * R), BF),
        vmem((TARGETS, 8, R), F32), vmem((X, TARGETS, 8, R), F32),
        vmem((2, R + EXTRA, R), I16), vmem((FRONTS, 2, R + EXTRA, R), I16),
        vmem((X, TARGETS, 2, R, R), F32),
        *[vmem((TARGETS, 2, R + EXTRA, R), I16)] * 6,
        vmem((TARGETS, 2, R, R), F32),
        vmem((2, 2 * R, 2 * R), BF),
        *ring,
        vmem((2, nz, 2, br + EXTRA, R), I16), vmem((2, tile, 2 * R), BF),
        vmem((TARGETS, R, 2 * R), F32), vmem((TARGETS, R, R), F32), vmem((2 * R, 2 * R), F32),
        vmem((X, TARGETS, 2 * R, 2 * R), BF), vmem((X, TARGETS, 2, R + EXTRA, R), I16),
        *ring,
        vmem((X, qr, 2 * R), F32),
        dma((X,)), dma((X,)), dma((X,)), dma((X,)), dma((X,)), dma((X,)), dma((X,)), dma((X,)),
        dma((X,)), dma((X,)), dma((X,)), dma((X,)), dma((6,)), dma((6,)),
        dma((nz,)), dma((nz,)), dma((4, np_)), dma((4, np_)),
        dma((4, np_)), dma((4, np_)), dma((nz, 2)), dma((nz, 2)),
        dma((6,)), dma((6,)),
        dma((nz,)), dma((nz,)), dma((4, np_)), dma((4, np_)),
        dma((X,)), dma((X,)),
    ]
    inside = pl.BlockSpec(memory_space=pltpu.VMEM)
    outside = pl.BlockSpec(memory_space=pltpu.HBM)
    out = jax.ShapeDtypeStruct((1, br, TARGETS, R), F32)
    return pl.pallas_call(
        functools.partial(kernel, rows, layers, tile),
        out_shape=(out, out),
        in_specs=[outside] * 5,
        out_specs=(inside, inside),
        scratch_shapes=scratch,
        compiler_params=pltpu.CompilerParams(
            collective_id=0, has_side_effects=True, vmem_limit_bytes=64 * 2**20
        ),
        name="trailing_update",
    )(panel_left, panel_right, test_matrix, ranks, offsets)


def solution(mesh):
    return jax.shard_map(
        on_device,
        mesh=mesh,
        in_specs=(
            P("row", "layer", None, None),
            P("row", "layer", None, None),
            P(),
            P("row", "layer"),
            P("row", None),
        ),
        out_specs=(P("row", "layer", None, None), P("row", "layer", None, None)),
        check_vma=False,
    )
```

```python
import functools

import jax
import jax.numpy as jnp
from jax import lax
from jax.experimental import pallas as pl
from jax.experimental.pallas import tpu as pltpu
from jax.sharding import PartitionSpec as P

R = 128
X = 4
FRONTS = 4
TARGETS = 2
BF = jnp.bfloat16
F32 = jnp.float32
HIGH = lax.Precision.HIGHEST


def dot(a, b, ca=1, cb=0, precision=None):
    return lax.dot_general(
        a, b, (((ca,), (cb,)), ((), ())), precision=precision, preferred_element_type=F32
    )


def split(a):
    high = a.astype(BF)
    return high, (a - high.astype(F32)).astype(BF)


EXTRA = 16
STEPS = 128.0
TOP = 32766.0


def coded(value, ref, *at):
    n = value.shape[0]
    most = jnp.maximum(jnp.max(jnp.abs(value), axis=0, keepdims=True), 1e-30)
    code = jnp.ceil(jnp.log2(most) * STEPS) + 1.0
    ref[(*at, slice(0, n), slice(None))] = (
        jnp.round(value * (TOP * jnp.exp2(code * (-1.0 / STEPS)))).astype(jnp.int32).astype(jnp.int16)
    )
    ref[(*at, slice(n, n + EXTRA), slice(None))] = (
        jnp.broadcast_to(code, (EXTRA, value.shape[1])).astype(jnp.int32).astype(jnp.int16)
    )


def decoded(ref, *at):
    n = ref.shape[-2] - EXTRA
    code = ref[(*at, slice(n, n + EXTRA), slice(None))].astype(jnp.int32).astype(F32)[0:1]
    steps = ref[(*at, slice(0, n), slice(None))].astype(jnp.int32).astype(F32)
    return steps * (jnp.exp2(code * (1.0 / STEPS)) * (1.0 / TOP))


def kernel(
    rows, layers, tile,
    u_hbm, v_hbm, test_hbm, ranks_hbm, offs_hbm,
    basis_ref, upd_ref,
    u_ref, v_ref, test_ref, ranks_ref, offs_ref, in_sem, unt, vt, un, um, vm, vq, uq, usel, meta, metas, probe_own, probes, parts, far_out, plain_out, chain_in, plain_in, sum_out, sum_in, core,
    mix, s_part, s_out, s_cx, s_send, s_recv, s_own, s_all, s_full, gx, linv, reach, wall, w_all, t_part, t_out, t_cx, t_send, t_recv, t_own, t_fin,
    a2v_s, a2v_r, a2u_s, a2u_r, yv_s, yv_r, yu_s, yu_r, mt_s, mt_r, pr_s, pr_r, cr_s, cr_r,
    scx_s, scx_r, srs_s, srs_r, ag_s, ag_r, agc_s, agc_r, wg_s, wg_r, tcx_s, tcx_r, trs_s, trs_r, fin_s, fin_r,
):
    ny, nz = rows // X, layers // 2
    np_, nm = nz // 2, nz - 1 - nz // 2
    br = tile // layers
    qr, hb = br // X, br // 2
    quarter = tile // X
    row, layer = lax.axis_index("row"), lax.axis_index("layer")
    x, y = lax.rem(row, X), lax.div(row, X)
    z, c = lax.div(layer, 2), lax.rem(layer, 2)

    def xdev(d):
        return (y * X + lax.rem(x + d, X), layer)

    def ydev(d):
        return (lax.rem(y + d + ny, ny) * X + x, layer)

    def zdev(d):
        return (row, lax.rem(z + d + nz, nz) * 2 + c)

    mate = (row, z * 2 + 1 - c)
    loads = [
        pltpu.make_async_copy(src, dst, in_sem.at[i])
        for i, (src, dst) in enumerate((
            (ranks_hbm, ranks_ref), (offs_hbm, offs_ref), (v_hbm, v_ref), (u_hbm, u_ref), (test_hbm, test_ref)))
    ]
    for load in loads:
        load.start()
    barrier = pltpu.get_barrier_semaphore()

    def zcross(d):
        return (row, lax.rem(z + d + nz, nz) * 2 + 1 - c)

    friends = [
        xdev(1), xdev(2), xdev(3), ydev(1), ydev(-1), zdev(1), zdev(-1), zcross(1), zcross(-1), mate]
    for friend in friends:
        pl.semaphore_signal(barrier, inc=1, device_id=friend, device_id_type=pl.DeviceIdType.MESH)

    def remote(src, dst, ssem, rsem, dev):
        return pltpu.make_async_remote_copy(
            src_ref=src, dst_ref=dst, send_sem=ssem, recv_sem=rsem,
            device_id=dev, device_id_type=pl.DeviceIdType.MESH,
        )

    pending = []

    def start(copy):
        copy.start()
        pending.append(copy)
        return copy

    loads[0].wait()
    loads[1].wait()
    lanes = lax.broadcasted_iota(jnp.int32, (1, R), 1)
    live = [(lanes < ranks_ref[0, k]).astype(F32).astype(BF) for k in range(2)]

    def mask_quarter(d):
        xx = lax.rem(x + d, X)

        def body(i, carry):
            src = pl.ds(pl.multiple_of(i * br + xx * qr, qr), qr)
            dst = pl.ds(pl.multiple_of(i * qr, qr), qr)
            for k in range(2):
                v = v_ref[0, k, src, :] * live[k]
                if d == 0:
                    vq[X + x, k, dst, :] = v
                else:
                    vm[xx, k, dst, :] = v
            return carry

        lax.fori_loop(0, layers, body, 0)

    def slot_of(d):
        return lax.rem(x - d + X, X)

    def a2a(d, src, dst, ss, rs):
        return remote(src.at[lax.rem(x + d, X)], dst.at[X + x], ss.at[d], rs.at[d], xdev(d))

    def ysend(d, buf, ss, rs):
        return remote(buf.at[X + slot_of(d)], buf.at[slot_of(d)], ss.at[d], rs.at[d], ydev(1))

    yv = [ysend(d, vq, yv_s, yv_r) for d in range(X)]
    av = [None] + [a2a(d, vm, vq, a2v_s, a2v_r) for d in (1, 2, 3)]
    loads[2].wait()
    mask_quarter(0)
    pl.semaphore_wait(barrier, len(friends))
    start(yv[0])
    mask_quarter(1)
    start(av[1])
    mask_quarter(3)
    start(av[3])
    mask_quarter(2)
    for s in range(TARGETS):
        meta[s, :, :] = jnp.full((8, R), offs_ref[0, s], jnp.int32).astype(F32)
    metas[x] = meta[...]
    mts = {d: start(remote(meta, metas.at[x], mt_s.at[d], mt_r.at[d], xdev(d))) for d in (1, 2, 3)}
    loads[3].wait()
    loads[4].wait()

    def mask_left(i, carry):
        src = pl.ds(pl.multiple_of(i * br, br), br)
        for k in range(2):
            u = u_ref[0, k, src, :] * live[k]
            un[k, src, :] = u
            unt[k * R:(k + 1) * R, src] = u.T
            for xx in range(X):
                um[xx, k, pl.ds(pl.multiple_of(i * qr, qr), qr), :] = u[xx * qr:(xx + 1) * qr]
        return carry

    lax.fori_loop(0, layers, mask_left, 0)
    uq[X + x] = um[x]
    probed = dot(unt[...], test_ref[...])
    for k in range(2):
        coded(probed[k * R:(k + 1) * R], probe_own, k)
    pry = start(remote(probe_own, probes.at[FRONTS - 1], pr_s.at[0], pr_r.at[0], ydev(1)))
    for d in (1, 3):
        av[d].wait_recv()
        start(yv[d])
    start(av[2])

    def probe_send(d, src):
        return remote(src, probes.at[d - 1], pr_s.at[d], pr_r.at[d], xdev(d))

    for d in (1, 2, 3):
        @pl.when(x + d < X)
        def _(d=d):
            probe_send(d, probe_own).start()
    for k in range(2):
        vt[k, pl.ds(pl.multiple_of(x * R, R), R), :] = vq[X + x, k].T
        for d in (1, 3):
            j = slot_of(d)
            vt[k, pl.ds(pl.multiple_of(j * R, R), R), :] = vq[X + j, k].T
    pry.wait_recv()
    for d in (1, 2, 3):
        @pl.when(x + d >= X)
        def _(d=d):
            probe_send(d, probes.at[FRONTS - 1]).start()
    prx = [probe_send(d, probe_own) for d in (1, 2, 3)]
    pending.extend(prx)
    av[2].wait_recv()
    start(yv[2])
    au = {d: a2a(d, um, uq, a2u_s, a2u_r) for d in (1, 2, 3)}
    start(au[1])
    start(au[3])
    for k in range(2):
        vt[k, pl.ds(pl.multiple_of(lax.rem(x + 2, X) * R, R), R), :] = vq[X + lax.rem(x + 2, X), k].T
    for copy in mts.values():
        copy.wait_recv()

    marks = [[metas[xx, s, 0:1, :] for s in range(TARGETS)] for xx in range(X)]
    parts[...] = jnp.zeros_like(parts)

    def add_cores(slot, first, back):
        for k in range(2):
            found = dot(vt[k, first * R:, :], vq[slot, k])
            for xx in range(first, X):
                block = found[(xx - first) * R:(xx - first + 1) * R]
                for s in range(TARGETS):
                    parts[xx, s, k] += block * (marks[xx][s] == back(xx)).astype(F32)

    for j in range(X - 1):
        add_cores(X + j, j + 1, lambda xx: float(xx - j))
    yu = [ysend(d, uq, yu_s, yu_r) for d in range(X)]
    for d in (0, 1, 3, 2):
        yv[d].wait_recv()
        j = slot_of(d)
        if d == 2:
            start(yu[0])
        add_cores(j, 0, lambda xx: (X + xx - j).astype(F32))

    far = lax.rem(x + 2, X)
    right, left = lax.rem(x + 1, X), lax.rem(x + 3, X)
    def code_part(who, s):
        for k in range(2):
            coded(parts[who, s, k], far_out if who is far else plain_out, s, k)

    code_part(far, 0)
    far0 = start(remote(far_out.at[0], chain_in.at[0], cr_s.at[0], cr_r.at[0], xdev(3)))
    code_part(far, 1)
    far1 = start(remote(far_out.at[1], chain_in.at[1], cr_s.at[1], cr_r.at[1], xdev(1)))
    code_part(right, 0)
    plain0 = start(remote(plain_out.at[0], plain_in.at[0], cr_s.at[2], cr_r.at[2], xdev(1)))
    code_part(left, 1)
    plain1 = start(remote(plain_out.at[1], plain_in.at[1], cr_s.at[3], cr_r.at[3], xdev(3)))
    far0.wait_recv()
    for k in range(2):
        coded(parts[left, 0, k] + decoded(chain_in, 0, k), sum_out, 0, k)
    sum0 = start(remote(sum_out.at[0], sum_in.at[0], cr_s.at[4], cr_r.at[4], xdev(3)))
    far1.wait_recv()
    for k in range(2):
        coded(parts[right, 1, k] + decoded(chain_in, 1, k), sum_out, 1, k)
    sum1 = start(remote(sum_out.at[1], sum_in.at[1], cr_s.at[5], cr_r.at[5], xdev(1)))
    for copy in prx:
        copy.wait_recv()
    plain0.wait_recv()
    plain1.wait_recv()
    sum0.wait_recv()
    sum1.wait_recv()
    for s in range(TARGETS):
        for k in range(2):
            core[s, k] = parts[x, s, k] + decoded(plain_in, s, k) + decoded(sum_in, s, k)

    start(au[2])
    for d in (1, 3):
        au[d].wait_recv()
        start(yu[d])

    for s in range(TARGETS):
        for k in range(2):
            back = jnp.clip(offs_ref[0, s] - 1, 0, FRONTS - 1)
            mixed = dot(core[s, k], decoded(probes, back, k), precision=HIGH)
            high, low = split(mixed)
            mix[0, k * R:(k + 1) * R, s * R:(s + 1) * R] = high
            mix[1, k * R:(k + 1) * R, s * R:(s + 1) * R] = low

    def order(i):
        half = lax.div(i + 1, 2)
        off = jnp.where(lax.rem(i, 2) == 1, half - np_, np_ - half)
        return lax.rem(z + off + nz, nz)

    def pair_copy(out, cx, ss, rs, zz):
        return remote(out.at[zz], cx.at[zz], ss.at[zz], rs.at[zz], mate)

    def sketch_rows(i, carry):
        zz = order(i)
        src = pl.ds(pl.multiple_of(zz * 2 * br, 2 * br), 2 * br)
        both = jnp.concatenate([un[0, src, :], un[1, src, :]], axis=1)
        got = dot(both, mix[0]) + dot(both, mix[1])
        s_part[0, zz] = got[:br]
        s_part[1, zz] = got[br:]
        for s in range(TARGETS):
            coded(s_part[1 - c, zz, :, s * R:(s + 1) * R], s_out, zz, s)
        pair_copy(s_out, s_cx, scx_s, scx_r, zz).start()
        return carry

    chains = [(1, 0, np_), (-1, 0, nm), (1, 1, nm), (-1, 1, np_)]
    groups = ((0, 3), (1, 2))

    def ring_reduce(part, out, cx, send, recv, ss_cx, rs_cx, ss, rs, own, before, between):
        waited = set()

        def term(off, h):
            zz = lax.rem(z + off + 2 * nz, nz)
            if off % nz not in waited:
                waited.add(off % nz)
                pair_copy(out, cx, ss_cx, rs_cx, zz).wait_recv()
            return part[c, zz, :, h * R:(h + 1) * R] + decoded(cx, zz, h)

        def hop(ch, i):
            return remote(send.at[ch, i], recv.at[ch, i], ss.at[ch, i], rs.at[ch, i], zdev(chains[ch][0]))

        before(0)
        for i in range(np_):
            for group in groups:
                if i == 0 and group is groups[1] and np_ > 1:
                    before(1)
                for ch in group:
                    sgn, h, n = chains[ch]
                    if i >= n:
                        continue
                    value = term(sgn * (n - i), h)
                    if i > 0:
                        hop(ch, i - 1).wait_recv()
                        value = value + decoded(recv, ch, i - 1)
                    coded(value, send, ch, i)
                    start(hop(ch, i))
                between()
            if i + 2 < np_:
                before(i + 2)
        for h in range(2):
            value = term(0, h)
            for ch, (sgn, hh, n) in enumerate(chains):
                if hh == h and n > 0:
                    hop(ch, n - 1).wait_recv()
                    value = value + decoded(recv, ch, n - 1)
            own[:, h * R:(h + 1) * R] = value

    def sketch_more(i):
        lax.fori_loop(max(2 * i - 1, 0), nz if i == np_ - 1 else 2 * i + 1, sketch_rows, 0)

    ring_reduce(
        s_part, s_out, s_cx, s_send, s_recv, scx_s, scx_r, srs_s, srs_r, s_own, sketch_more, lambda: None)
    au[2].wait_recv()
    start(yu[2])

    for h in range(2):
        coded(s_own[:, h * R:(h + 1) * R], s_all, c, z, h)

    def gather_hop(ch, i):
        sgn, h, n = chains[ch]
        zz = lax.rem(z - sgn * i + nz, nz)
        return remote(s_all.at[c, zz, h], s_all.at[c, zz, h], ag_s.at[ch, i], ag_r.at[ch, i], zdev(sgn))

    def to_mate(off, h):
        zz = lax.rem(z + off + nz, nz)
        at = (off + nz) % nz
        return remote(s_all.at[c, zz, h], s_all.at[c, zz, h], agc_s.at[at, h], agc_r.at[at, h], mate)

    def spread(par, off, h):
        zz = lax.rem(z + off + nz, nz)
        high, low = split(decoded(s_all, par, zz, h))
        to = pl.ds(pl.multiple_of((zz * 2 + par) * br, br), br)
        s_full[0, to, h * R:(h + 1) * R] = high
        s_full[1, to, h * R:(h + 1) * R] = low

    def launch(ch, i):
        sgn, h, n = chains[ch]
        start(gather_hop(ch, i))
        if n == np_ and i == n - 1:
            zz = lax.rem(z - sgn * i + nz, nz)
            at = (-sgn * n) % nz
            start(remote(s_all.at[c, zz, h], s_all.at[c, zz, h], agc_s.at[at, h], agc_r.at[at, h], zcross(sgn)))

    def use(off):
        zz = lax.rem(z + off + nz, nz)
        src = pl.ds(pl.multiple_of(zz * 2 * br, 2 * br), 2 * br)
        reach[...] += dot(unt[:, src], s_full[0, src, :]) + dot(unt[:, src], s_full[1, src, :])
        for s in range(TARGETS):
            at = slice(s * R, (s + 1) * R)
            high, low = s_full[0, src, at], s_full[1, src, at]
            gx[s] += dot(high, jnp.concatenate([high, low], axis=1), 0, 0)

    for ch in groups[0]:
        launch(ch, 0)
    reach[...] = jnp.zeros_like(reach)
    gx[...] = jnp.zeros_like(gx)
    for h in range(2):
        spread(c, 0, h)
    for ch in groups[1]:
        if chains[ch][2] > 0:
            launch(ch, 0)
    for h in range(2):
        start(to_mate(0, h))
    late = [(0, h) for h in range(2)]
    for i in range(np_):
        got = []
        ready = sorted({i, -i})
        for group in groups:
            for ch in group:
                sgn, h, n = chains[ch]
                if i < n:
                    gather_hop(ch, i).wait_recv()
                    if i + 1 < n:
                        launch(ch, i + 1)
                    off = -sgn * (i + 1)
                    if i < np_ - 1:
                        start(to_mate(off, h))
                    got.append((off, h))
            if group is groups[0]:
                for off, h in late:
                    to_mate(off, h).wait_recv()
                    spread(1 - c, off, h)
                use(ready[0])
            else:
                for off, h in got:
                    spread(c, off, h)
                for off in ready[1:]:
                    use(off)
        late = got
    for off, h in late:
        to_mate(off, h).wait_recv()
        spread(1 - c, off, h)
    use(np_)

    pick16 = [[[(marks[xx][s] == o).astype(F32).astype(BF) for o in range(1, FRONTS + 1)]
               for s in range(TARGETS)] for xx in range(X)]

    def choose_rows(i, carry):
        src = pl.ds(pl.multiple_of(i * 32, 32), 32)
        for xx in range(X):
            for k in range(2):
                cand = [uq[X + xx - o, k, src, :] for o in range(1, FRONTS + 1)]
                for s in range(TARGETS):
                    total = cand[0] * pick16[xx][s][0]
                    for o in range(1, FRONTS):
                        total = total + cand[o] * pick16[xx][s][o]
                    usel[xx, s, src, k * R:(k + 1) * R] = total
        return carry

    for s in range(TARGETS):
        for k in range(2):
            weight = dot(core[s, k], reach[k * R:(k + 1) * R, s * R:(s + 1) * R], 0, 0, precision=HIGH)
            coded(weight, w_all, x, s, k)
            high, low = split(weight)
            wall[x, s, k * R:(k + 1) * R, 0:R] = high
            wall[x, s, k * R:(k + 1) * R, R:2 * R] = low

    def weight_send(i, who, s, d):
        return remote(w_all.at[who, s], w_all.at[who, s], wg_s.at[i], wg_r.at[i], xdev(d))

    wr1 = start(weight_send(0, x, 1, 1))
    wl0 = start(weight_send(1, x, 0, 3))
    wr0 = start(weight_send(2, x, 0, 1))
    wl1 = start(weight_send(3, x, 1, 3))

    eye = (lax.broadcasted_iota(jnp.int32, (R, R), 0) == lax.broadcasted_iota(jnp.int32, (R, R), 1)).astype(F32)
    for s in range(TARGETS):
        cross = gx[s, :, R:2 * R]
        gx[s, :, 0:R] = (gx[s, :, 0:R] + (cross + cross.T)) / tile
        gx[s, :, R:2 * R] = eye

    lane8 = lax.broadcasted_iota(jnp.int32, (8, R), 1)
    sub8 = lax.broadcasted_iota(jnp.int32, (8, R), 0)

    def factor_block(b, carry):
        r0 = pl.multiple_of(b * 8, 8)
        for s in range(TARGETS):
            gg = gx[s, pl.ds(r0, 8), 0:R]
            xx = gx[s, pl.ds(r0, 8), R:2 * R]
            cols = [
                jnp.broadcast_to(
                    jnp.sum(jnp.where(lane8 == r0 + j, gg, 0.0), axis=1, keepdims=True), (8, R))
                for j in range(8)
            ]
            diag = jnp.ones((8, R), F32)
            for j in range(8):
                pivot = cols[j][j:j + 1]
                diag = jnp.where(sub8 == j, pivot, diag)
                f = jnp.where(sub8 > j, cols[j] / pivot, 0.0)
                for m in range(j + 1, 8):
                    cols[m] = cols[m] - f * cols[m][j:j + 1]
                gg = gg - f * gg[j:j + 1]
                xx = xx - f * xx[j:j + 1]
            linv[s, pl.ds(r0, 8), :] = xx / jnp.sqrt(diag)
            lead = jnp.where(lane8 >= r0 + 8, gg / diag, 0.0)
            gx[s] -= dot(lead, jnp.concatenate([gg, xx], axis=1), 0, 0, precision=HIGH)
        return carry

    blocks = R // 8
    lax.fori_loop(0, blocks // 4, factor_block, 0)
    wr1.wait_recv()
    fr1 = start(weight_send(4, left, 1, 1))
    wl0.wait_recv()
    fl0 = start(weight_send(5, right, 0, 3))

    for d in range(X):
        yu[d].wait_recv()
    lax.fori_loop(0, quarter // 32, choose_rows, 0)
    for copy in (wr0, wl1, fr1, fl0):
        copy.wait_recv()
    for d in (1, 2, 3):
        who = lax.rem(x + d, X)
        for s in range(TARGETS):
            for k in range(2):
                high, low = split(decoded(w_all, who, s, k))
                wall[who, s, k * R:(k + 1) * R, 0:R] = high
                wall[who, s, k * R:(k + 1) * R, R:2 * R] = low

    span = layers // 2
    for q in range(2):
        src = slice(q * span * qr, (q + 1) * span * qr)
        for xx in range(X):
            for s in range(TARGETS):
                got = dot(usel[xx, s, src, :], wall[xx, s])
                got = got[:, 0:R] + got[:, R:2 * R]
                for i in range(span):
                    t_part[i % 2, (q * span + i) // 2, xx * qr:(xx + 1) * qr, s * R:(s + 1) * R] = got[i * qr:(i + 1) * qr]
        for zz in range(q * nz // 2, (q + 1) * nz // 2):
            for s in range(TARGETS):
                coded(t_part[1 - c, zz, :, s * R:(s + 1) * R], t_out, zz, s)
            pair_copy(t_out, t_cx, tcx_s, tcx_r, zz).start()
    factored = [blocks // 4]

    def factor_more(count=1):
        upto = min(factored[0] + count, blocks)
        lax.fori_loop(factored[0], upto, factor_block, 0)
        factored[0] = upto

    factor_more(2)
    ring_reduce(t_part, t_out, t_cx, t_send, t_recv, tcx_s, tcx_r, trs_s, trs_r, t_own, lambda i: None, factor_more)

    def final_send(d):
        at = pl.ds(pl.multiple_of(lax.rem(x + d, X) * qr, qr), qr)
        return remote(t_own.at[at, :], t_fin.at[x], fin_s.at[d], fin_r.at[d], xdev(d))

    fins = [start(final_send(d)) for d in (2, 1, 3)]
    t_fin[x] = t_own[pl.ds(pl.multiple_of(x * qr, qr), qr), :]
    factor_more(blocks)
    for s in range(TARGETS):
        at = slice(s * R, (s + 1) * R)
        basis_ref[0, :, s, :] = dot(s_own[:, at], linv[s], 1, 1, precision=HIGH)
    for copy in fins:
        copy.wait_recv()
    for s in range(TARGETS):
        at = slice(s * R, (s + 1) * R)
        terms = jnp.concatenate([t_fin[i, :, at] for i in range(X)], axis=0)
        upd_ref[0, :, s, :] = dot(terms, linv[s], 1, 1, precision=HIGH) / tile

    for copy in pending:
        copy.wait_send()

    def pair_end(zz, carry):
        pair_copy(s_out, s_cx, scx_s, scx_r, zz).wait_send()
        pair_copy(t_out, t_cx, tcx_s, tcx_r, zz).wait_send()
        return carry

    lax.fori_loop(0, nz, pair_end, 0)


def on_device(panel_left, panel_right, test_matrix, ranks, offsets):
    rows, layers = lax.axis_size("row"), lax.axis_size("layer")
    tile = panel_left.shape[2]
    nz = layers // 2
    np_ = max(nz // 2, 1)
    br = tile // layers
    qr, hb, quarter = br // X, br // 2, tile // X
    dma = pltpu.SemaphoreType.DMA
    vmem = pltpu.VMEM
    I16 = jnp.int16
    ring = [
        vmem((2, nz, br, 2 * R), F32), vmem((nz, 2, br + EXTRA, R), I16), vmem((nz, 2, br + EXTRA, R), I16),
        vmem((4, np_, br + EXTRA, R), I16), vmem((4, np_, br + EXTRA, R), I16), vmem((br, 2 * R), F32),
    ]
    scratch = [
        vmem((1, 2, tile, R), BF), vmem((1, 2, tile, R), BF), vmem((tile, R), BF),
        pltpu.SMEM((1, 2), jnp.int32), pltpu.SMEM((1, TARGETS), jnp.int32), dma((5,)),
        vmem((2 * R, tile), BF), vmem((2, X * R, quarter), BF),
        vmem((2, tile, R), BF), vmem((X, 2, quarter, R), BF), vmem((X, 2, quarter, R), BF),
        vmem((2 * X, 2, quarter, R), BF), vmem((2 * X, 2, quarter, R), BF),
        vmem((X, TARGETS, quarter, 2 * R), BF),
        vmem((TARGETS, 8, R), F32), vmem((X, TARGETS, 8, R), F32),
        vmem((2, R + EXTRA, R), I16), vmem((FRONTS, 2, R + EXTRA, R), I16),
        vmem((X, TARGETS, 2, R, R), F32),
        *[vmem((TARGETS, 2, R + EXTRA, R), I16)] * 6,
        vmem((TARGETS, 2, R, R), F32),
        vmem((2, 2 * R, 2 * R), BF),
        *ring,
        vmem((2, nz, 2, br + EXTRA, R), I16), vmem((2, tile, 2 * R), BF),
        vmem((TARGETS, R, 2 * R), F32), vmem((TARGETS, R, R), F32), vmem((2 * R, 2 * R), F32),
        vmem((X, TARGETS, 2 * R, 2 * R), BF), vmem((X, TARGETS, 2, R + EXTRA, R), I16),
        *ring,
        vmem((X, qr, 2 * R), F32),
        dma((X,)), dma((X,)), dma((X,)), dma((X,)), dma((X,)), dma((X,)), dma((X,)), dma((X,)),
        dma((X,)), dma((X,)), dma((X,)), dma((X,)), dma((6,)), dma((6,)),
        dma((nz,)), dma((nz,)), dma((4, np_)), dma((4, np_)),
        dma((4, np_)), dma((4, np_)), dma((nz, 2)), dma((nz, 2)),
        dma((6,)), dma((6,)),
        dma((nz,)), dma((nz,)), dma((4, np_)), dma((4, np_)),
        dma((X,)), dma((X,)),
    ]
    inside = pl.BlockSpec(memory_space=pltpu.VMEM)
    outside = pl.BlockSpec(memory_space=pltpu.HBM)
    out = jax.ShapeDtypeStruct((1, br, TARGETS, R), F32)
    return pl.pallas_call(
        functools.partial(kernel, rows, layers, tile),
        out_shape=(out, out),
        in_specs=[outside] * 5,
        out_specs=(inside, inside),
        scratch_shapes=scratch,
        compiler_params=pltpu.CompilerParams(
            collective_id=0, has_side_effects=True, vmem_limit_bytes=64 * 2**20
        ),
        name="trailing_update",
    )(panel_left, panel_right, test_matrix, ranks, offsets)


def solution(mesh):
    return jax.shard_map(
        on_device,
        mesh=mesh,
        in_specs=(
            P("row", "layer", None, None),
            P("row", "layer", None, None),
            P(),
            P("row", "layer"),
            P("row", None),
        ),
        out_specs=(P("row", "layer", None, None), P("row", "layer", None, None)),
        check_vma=False,
    )
```

```python
import functools

import jax
import jax.numpy as jnp
from jax import lax
from jax.experimental import pallas as pl
from jax.experimental.pallas import tpu as pltpu
from jax.sharding import PartitionSpec as P

R = 128
X = 4
FRONTS = 4
TARGETS = 2
BF = jnp.bfloat16
F32 = jnp.float32
HIGH = lax.Precision.HIGHEST


def dot(a, b, ca=1, cb=0, precision=None):
    return lax.dot_general(
        a, b, (((ca,), (cb,)), ((), ())), precision=precision, preferred_element_type=F32
    )


def split(a):
    high = a.astype(BF)
    return high, (a - high.astype(F32)).astype(BF)


EXTRA = 16
STEPS = 128.0
TOP = 32766.0


def coded(value, ref, *at):
    n = value.shape[0]
    most = jnp.maximum(jnp.max(jnp.abs(value), axis=0, keepdims=True), 1e-30)
    code = jnp.ceil(jnp.log2(most) * STEPS) + 1.0
    ref[(*at, slice(0, n), slice(None))] = (
        jnp.round(value * (TOP * jnp.exp2(code * (-1.0 / STEPS)))).astype(jnp.int32).astype(jnp.int16)
    )
    ref[(*at, slice(n, n + EXTRA), slice(None))] = (
        jnp.broadcast_to(code, (EXTRA, value.shape[1])).astype(jnp.int32).astype(jnp.int16)
    )


def decoded(ref, *at):
    n = ref.shape[-2] - EXTRA
    code = ref[(*at, slice(n, n + EXTRA), slice(None))].astype(jnp.int32).astype(F32)[0:1]
    steps = ref[(*at, slice(0, n), slice(None))].astype(jnp.int32).astype(F32)
    return steps * (jnp.exp2(code * (1.0 / STEPS)) * (1.0 / TOP))


def kernel(
    rows, layers, tile,
    u_hbm, v_hbm, test_hbm, ranks_hbm, offs_hbm,
    basis_ref, upd_ref,
    u_ref, v_ref, test_ref, ranks_ref, offs_ref, in_sem, unt, vt, un, um, vm, vq, uq, usel, meta, metas, probe_own, probes, parts, far_out, plain_out, chain_in, plain_in, sum_out, sum_in, core,
    mix, s_part, s_out, s_cx, s_send, s_recv, s_own, s_all, s_full, gx, linv, reach, wall, w_all, t_part, t_out, t_cx, t_send, t_recv, t_own, t_fin,
    a2v_s, a2v_r, a2u_s, a2u_r, yv_s, yv_r, yu_s, yu_r, mt_s, mt_r, pr_s, pr_r, cr_s, cr_r,
    scx_s, scx_r, srs_s, srs_r, ag_s, ag_r, agc_s, agc_r, wg_s, wg_r, tcx_s, tcx_r, trs_s, trs_r, fin_s, fin_r,
):
    ny, nz = rows // X, layers // 2
    np_, nm = nz // 2, nz - 1 - nz // 2
    br = tile // layers
    qr, hb = br // X, br // 2
    quarter = tile // X
    row, layer = lax.axis_index("row"), lax.axis_index("layer")
    x, y = lax.rem(row, X), lax.div(row, X)
    z, c = lax.div(layer, 2), lax.rem(layer, 2)

    def xdev(d):
        return (y * X + lax.rem(x + d, X), layer)

    def ydev(d):
        return (lax.rem(y + d + ny, ny) * X + x, layer)

    def zdev(d):
        return (row, lax.rem(z + d + nz, nz) * 2 + c)

    mate = (row, z * 2 + 1 - c)
    loads = [
        pltpu.make_async_copy(src, dst, in_sem.at[i])
        for i, (src, dst) in enumerate((
            (ranks_hbm, ranks_ref), (offs_hbm, offs_ref), (v_hbm, v_ref), (u_hbm, u_ref), (test_hbm, test_ref)))
    ]
    for load in loads:
        load.start()
    barrier = pltpu.get_barrier_semaphore()

    def zcross(d):
        return (row, lax.rem(z + d + nz, nz) * 2 + 1 - c)

    friends = [
        xdev(1), xdev(2), xdev(3), ydev(1), ydev(-1), zdev(1), zdev(-1), zcross(1), zcross(-1), mate]
    for friend in friends:
        pl.semaphore_signal(barrier, inc=1, device_id=friend, device_id_type=pl.DeviceIdType.MESH)

    def remote(src, dst, ssem, rsem, dev):
        return pltpu.make_async_remote_copy(
            src_ref=src, dst_ref=dst, send_sem=ssem, recv_sem=rsem,
            device_id=dev, device_id_type=pl.DeviceIdType.MESH,
        )

    pending = []

    def start(copy):
        copy.start()
        pending.append(copy)
        return copy

    loads[0].wait()
    loads[1].wait()
    lanes = lax.broadcasted_iota(jnp.int32, (1, R), 1)
    live = [(lanes < ranks_ref[0, k]).astype(F32).astype(BF) for k in range(2)]

    def mask_quarter(d):
        xx = lax.rem(x + d, X)

        def body(i, carry):
            src = pl.ds(pl.multiple_of(i * br + xx * qr, qr), qr)
            dst = pl.ds(pl.multiple_of(i * qr, qr), qr)
            for k in range(2):
                v = v_ref[0, k, src, :] * live[k]
                if d == 0:
                    vq[X + x, k, dst, :] = v
                else:
                    vm[xx, k, dst, :] = v
            return carry

        lax.fori_loop(0, layers, body, 0)

    def slot_of(d):
        return lax.rem(x - d + X, X)

    def a2a(d, src, dst, ss, rs):
        return remote(src.at[lax.rem(x + d, X)], dst.at[X + x], ss.at[d], rs.at[d], xdev(d))

    def ysend(d, buf, ss, rs):
        return remote(buf.at[X + slot_of(d)], buf.at[slot_of(d)], ss.at[d], rs.at[d], ydev(1))

    yv = {
        (d, k): remote(
            vq.at[X + slot_of(d), k], vq.at[slot_of(d), k], yv_s.at[d, k], yv_r.at[d, k], ydev(1))
        for d in range(X) for k in range(2)
    }
    av = {
        (d, k): remote(
            vm.at[lax.rem(x + d, X), k], vq.at[X + x, k], a2v_s.at[d, k], a2v_r.at[d, k], xdev(d))
        for d in (1, 2, 3) for k in range(2)
    }
    loads[2].wait()
    mask_quarter(0)
    pl.semaphore_wait(barrier, len(friends))
    start(yv[0, 0])
    start(yv[0, 1])
    mask_quarter(1)
    start(av[1, 0])
    mask_quarter(3)
    start(av[3, 0])
    start(av[1, 1])
    start(av[3, 1])
    mask_quarter(2)
    for s in range(TARGETS):
        meta[s, :, :] = jnp.full((8, R), offs_ref[0, s], jnp.int32).astype(F32)
    metas[x] = meta[...]
    mts = {d: start(remote(meta, metas.at[x], mt_s.at[d], mt_r.at[d], xdev(d))) for d in (1, 2, 3)}
    loads[3].wait()
    loads[4].wait()

    def mask_left(i, carry):
        src = pl.ds(pl.multiple_of(i * br, br), br)
        for k in range(2):
            u = u_ref[0, k, src, :] * live[k]
            un[k, src, :] = u
            unt[k * R:(k + 1) * R, src] = u.T
            for xx in range(X):
                um[xx, k, pl.ds(pl.multiple_of(i * qr, qr), qr), :] = u[xx * qr:(xx + 1) * qr]
        return carry

    lax.fori_loop(0, layers, mask_left, 0)
    uq[X + x] = um[x]
    probed = dot(unt[...], test_ref[...])
    for k in range(2):
        coded(probed[k * R:(k + 1) * R], probe_own, k)
    pry = start(remote(probe_own, probes.at[FRONTS - 1], pr_s.at[0], pr_r.at[0], ydev(1)))
    for d in (1, 3):
        av[d, 0].wait_recv()
        start(yv[d, 0])
    start(av[2, 0])

    def probe_send(d, src):
        return remote(src, probes.at[d - 1], pr_s.at[d], pr_r.at[d], xdev(d))

    for d in (1, 2, 3):
        @pl.when(x + d < X)
        def _(d=d):
            probe_send(d, probe_own).start()
    def turn(d, k):
        j = slot_of(d)
        vt[k, pl.ds(pl.multiple_of(j * R, R), R), :] = vq[X + j, k].T

    turn(0, 0)
    turn(0, 1)
    turn(1, 0)
    turn(3, 0)
    av[2, 0].wait_recv()
    start(yv[2, 0])
    start(av[2, 1])
    turn(2, 0)
    pry.wait_recv()
    for d in (1, 2, 3):
        @pl.when(x + d >= X)
        def _(d=d):
            probe_send(d, probes.at[FRONTS - 1]).start()
    prx = [probe_send(d, probe_own) for d in (1, 2, 3)]
    pending.extend(prx)
    au = {d: a2a(d, um, uq, a2u_s, a2u_r) for d in (1, 2, 3)}
    for copy in mts.values():
        copy.wait_recv()

    marks = [[metas[xx, s, 0:1, :] for s in range(TARGETS)] for xx in range(X)]
    parts[...] = jnp.zeros_like(parts)

    def add_cores(k, slot, first, back):
        found = dot(vt[k, first * R:, :], vq[slot, k])
        for xx in range(first, X):
            block = found[(xx - first) * R:(xx - first + 1) * R]
            for s in range(TARGETS):
                parts[xx, s, k] += block * (marks[xx][s] == back(xx)).astype(F32)

    def add_same(k):
        for j in range(X - 1):
            add_cores(k, X + j, j + 1, lambda xx: float(xx - j))

    def add_arrived(d, k):
        yv[d, k].wait_recv()
        j = slot_of(d)
        add_cores(k, j, 0, lambda xx: (X + xx - j).astype(F32))

    far = lax.rem(x + 2, X)
    right, left = lax.rem(x + 1, X), lax.rem(x + 3, X)

    def core_hop(i, k, out, into, s, d):
        return remote(out.at[s, k], into.at[s, k], cr_s.at[i, k], cr_r.at[i, k], xdev(d))

    trips = [(far, far_out, chain_in, s, 2) for s in range(2)]
    trips += [(right, plain_out, plain_in, s, 1) for s in range(2)] + [(left, sum_out, sum_in, s, 3) for s in range(2)]

    def cores_out(k):
        for i, (who, out, into, s, d) in enumerate(trips):
            coded(parts[who, s, k], out, s, k)
            start(core_hop(i, k, out, into, s, d))

    def cores_in(k):
        for i, (who, out, into, s, d) in enumerate(trips):
            core_hop(i, k, out, into, s, d).wait_recv()
        for s in range(TARGETS):
            core[s, k] = (
                parts[x, s, k] + decoded(chain_in, s, k) + decoded(plain_in, s, k) + decoded(sum_in, s, k))

    def mix_layer(k):
        for s in range(TARGETS):
            back = jnp.clip(offs_ref[0, s] - 1, 0, FRONTS - 1)
            mixed = dot(core[s, k], decoded(probes, back, k), precision=HIGH)
            high, low = split(mixed)
            mix[0, k * R:(k + 1) * R, s * R:(s + 1) * R] = high
            mix[1, k * R:(k + 1) * R, s * R:(s + 1) * R] = low

    yu = [ysend(d, uq, yu_s, yu_r) for d in range(X)]
    add_same(0)
    for d in (0, 1, 3):
        add_arrived(d, 0)
    av[1, 1].wait_recv()
    start(yv[1, 1])
    av[3, 1].wait_recv()
    turn(1, 1)
    turn(3, 1)
    yv[2, 0].wait_recv()
    start(yv[3, 1])
    av[2, 1].wait_recv()
    start(yv[2, 1])
    last = slot_of(2)
    add_cores(0, last, 0, lambda xx: (X + xx - last).astype(F32))
    cores_out(0)
    turn(2, 1)
    add_same(1)
    start(au[1])
    start(au[3])
    add_arrived(0, 1)
    add_arrived(1, 1)
    for copy in prx:
        copy.wait_recv()
    cores_in(0)
    mix_layer(0)
    add_arrived(3, 1)
    yv[2, 1].wait_recv()
    start(yu[0])
    add_cores(1, last, 0, lambda xx: (X + xx - last).astype(F32))
    cores_out(1)
    cores_in(1)

    start(au[2])
    mix_layer(1)

    def order(i):
        half = lax.div(i + 1, 2)
        off = jnp.where(lax.rem(i, 2) == 1, half - np_, np_ - half)
        return lax.rem(z + off + nz, nz)

    def pair_copy(out, cx, ss, rs, zz):
        return remote(out.at[zz], cx.at[zz], ss.at[zz], rs.at[zz], mate)

    def sketch_rows(i, carry):
        zz = order(i)
        src = pl.ds(pl.multiple_of(zz * 2 * br, 2 * br), 2 * br)
        both = jnp.concatenate([un[0, src, :], un[1, src, :]], axis=1)
        got = dot(both, mix[0]) + dot(both, mix[1])
        s_part[0, zz] = got[:br]
        s_part[1, zz] = got[br:]
        for s in range(TARGETS):
            coded(s_part[1 - c, zz, :, s * R:(s + 1) * R], s_out, zz, s)
        pair_copy(s_out, s_cx, scx_s, scx_r, zz).start()
        return carry

    chains = [(1, 0, np_), (-1, 0, nm), (1, 1, nm), (-1, 1, np_)]
    groups = ((0, 3), (1, 2))

    def ring_reduce(part, out, cx, send, recv, ss_cx, rs_cx, ss, rs, own, before, between):
        waited = set()

        def term(off, h):
            zz = lax.rem(z + off + 2 * nz, nz)
            if off % nz not in waited:
                waited.add(off % nz)
                pair_copy(out, cx, ss_cx, rs_cx, zz).wait_recv()
            return part[c, zz, :, h * R:(h + 1) * R] + decoded(cx, zz, h)

        def hop(ch, i):
            return remote(send.at[ch, i], recv.at[ch, i], ss.at[ch, i], rs.at[ch, i], zdev(chains[ch][0]))

        before(0)
        for i in range(np_):
            for group in groups:
                if i == 0 and group is groups[1] and np_ > 1:
                    before(1)
                for ch in group:
                    sgn, h, n = chains[ch]
                    if i >= n:
                        continue
                    value = term(sgn * (n - i), h)
                    if i > 0:
                        hop(ch, i - 1).wait_recv()
                        value = value + decoded(recv, ch, i - 1)
                    coded(value, send, ch, i)
                    start(hop(ch, i))
                between()
            if i + 2 < np_:
                before(i + 2)
        for h in range(2):
            value = term(0, h)
            for ch, (sgn, hh, n) in enumerate(chains):
                if hh == h and n > 0:
                    hop(ch, n - 1).wait_recv()
                    value = value + decoded(recv, ch, n - 1)
            own[:, h * R:(h + 1) * R] = value

    def sketch_more(i):
        lax.fori_loop(max(2 * i - 1, 0), nz if i == np_ - 1 else 2 * i + 1, sketch_rows, 0)
        if i == min(1, np_ - 1):
            for d in (1, 3):
                au[d].wait_recv()
                start(yu[d])

    ring_reduce(
        s_part, s_out, s_cx, s_send, s_recv, scx_s, scx_r, srs_s, srs_r, s_own, sketch_more, lambda: None)
    au[2].wait_recv()
    start(yu[2])

    for h in range(2):
        coded(s_own[:, h * R:(h + 1) * R], s_all, c, z, h)

    def gather_hop(ch, i):
        sgn, h, n = chains[ch]
        zz = lax.rem(z - sgn * i + nz, nz)
        return remote(s_all.at[c, zz, h], s_all.at[c, zz, h], ag_s.at[ch, i], ag_r.at[ch, i], zdev(sgn))

    def to_mate(off, h):
        zz = lax.rem(z + off + nz, nz)
        at = (off + nz) % nz
        return remote(s_all.at[c, zz, h], s_all.at[c, zz, h], agc_s.at[at, h], agc_r.at[at, h], mate)

    def spread(par, off, h):
        zz = lax.rem(z + off + nz, nz)
        high, low = split(decoded(s_all, par, zz, h))
        to = pl.ds(pl.multiple_of((zz * 2 + par) * br, br), br)
        s_full[0, to, h * R:(h + 1) * R] = high
        s_full[1, to, h * R:(h + 1) * R] = low

    def launch(ch, i):
        sgn, h, n = chains[ch]
        start(gather_hop(ch, i))
        if n == np_ and i == n - 1:
            zz = lax.rem(z - sgn * i + nz, nz)
            at = (-sgn * n) % nz
            start(remote(s_all.at[c, zz, h], s_all.at[c, zz, h], agc_s.at[at, h], agc_r.at[at, h], zcross(sgn)))

    def use(off):
        zz = lax.rem(z + off + nz, nz)
        src = pl.ds(pl.multiple_of(zz * 2 * br, 2 * br), 2 * br)
        reach[...] += dot(unt[:, src], s_full[0, src, :]) + dot(unt[:, src], s_full[1, src, :])
        for s in range(TARGETS):
            at = slice(s * R, (s + 1) * R)
            high, low = s_full[0, src, at], s_full[1, src, at]
            gx[s] += dot(high, jnp.concatenate([high, low], axis=1), 0, 0)

    for ch in groups[0]:
        launch(ch, 0)
    reach[...] = jnp.zeros_like(reach)
    gx[...] = jnp.zeros_like(gx)
    for h in range(2):
        spread(c, 0, h)
    for ch in groups[1]:
        if chains[ch][2] > 0:
            launch(ch, 0)
    for h in range(2):
        start(to_mate(0, h))
    late = [(0, h) for h in range(2)]
    for i in range(np_):
        got = []
        ready = sorted({i, -i})
        for group in groups:
            for ch in group:
                sgn, h, n = chains[ch]
                if i < n:
                    gather_hop(ch, i).wait_recv()
                    if i + 1 < n:
                        launch(ch, i + 1)
                    off = -sgn * (i + 1)
                    if i < np_ - 1:
                        start(to_mate(off, h))
                    got.append((off, h))
            if group is groups[0]:
                for off, h in late:
                    to_mate(off, h).wait_recv()
                    spread(1 - c, off, h)
                use(ready[0])
            else:
                for off, h in got:
                    spread(c, off, h)
                for off in ready[1:]:
                    use(off)
        late = got
    for off, h in late:
        to_mate(off, h).wait_recv()
        spread(1 - c, off, h)
    use(np_)

    pick16 = [[[(marks[xx][s] == o).astype(F32).astype(BF) for o in range(1, FRONTS + 1)]
               for s in range(TARGETS)] for xx in range(X)]

    def choose_rows(i, carry):
        src = pl.ds(pl.multiple_of(i * 32, 32), 32)
        for xx in range(X):
            for k in range(2):
                cand = [uq[X + xx - o, k, src, :] for o in range(1, FRONTS + 1)]
                for s in range(TARGETS):
                    total = cand[0] * pick16[xx][s][0]
                    for o in range(1, FRONTS):
                        total = total + cand[o] * pick16[xx][s][o]
                    usel[xx, s, src, k * R:(k + 1) * R] = total
        return carry

    for s in range(TARGETS):
        for k in range(2):
            weight = dot(core[s, k], reach[k * R:(k + 1) * R, s * R:(s + 1) * R], 0, 0, precision=HIGH)
            coded(weight, w_all, x, s, k)
            high, low = split(weight)
            wall[x, s, k * R:(k + 1) * R, 0:R] = high
            wall[x, s, k * R:(k + 1) * R, R:2 * R] = low

    def weight_send(i, who, s, d):
        return remote(w_all.at[who, s], w_all.at[who, s], wg_s.at[i], wg_r.at[i], xdev(d))

    wr1 = start(weight_send(0, x, 1, 1))
    wl0 = start(weight_send(1, x, 0, 3))
    wr0 = start(weight_send(2, x, 0, 1))
    wl1 = start(weight_send(3, x, 1, 3))

    eye = (lax.broadcasted_iota(jnp.int32, (R, R), 0) == lax.broadcasted_iota(jnp.int32, (R, R), 1)).astype(F32)
    for s in range(TARGETS):
        cross = gx[s, :, R:2 * R]
        gx[s, :, 0:R] = (gx[s, :, 0:R] + (cross + cross.T)) / tile
        gx[s, :, R:2 * R] = eye

    lane8 = lax.broadcasted_iota(jnp.int32, (8, R), 1)
    sub8 = lax.broadcasted_iota(jnp.int32, (8, R), 0)

    def factor_block(b, carry):
        r0 = pl.multiple_of(b * 8, 8)
        for s in range(TARGETS):
            gg = gx[s, pl.ds(r0, 8), 0:R]
            xx = gx[s, pl.ds(r0, 8), R:2 * R]
            cols = [
                jnp.broadcast_to(
                    jnp.sum(jnp.where(lane8 == r0 + j, gg, 0.0), axis=1, keepdims=True), (8, R))
                for j in range(8)
            ]
            diag = jnp.ones((8, R), F32)
            for j in range(8):
                pivot = cols[j][j:j + 1]
                diag = jnp.where(sub8 == j, pivot, diag)
                f = jnp.where(sub8 > j, cols[j] / pivot, 0.0)
                for m in range(j + 1, 8):
                    cols[m] = cols[m] - f * cols[m][j:j + 1]
                gg = gg - f * gg[j:j + 1]
                xx = xx - f * xx[j:j + 1]
            linv[s, pl.ds(r0, 8), :] = xx / jnp.sqrt(diag)
            lead = jnp.where(lane8 >= r0 + 8, gg / diag, 0.0)
            gx[s] -= dot(lead, jnp.concatenate([gg, xx], axis=1), 0, 0, precision=HIGH)
        return carry

    blocks = R // 8
    lax.fori_loop(0, blocks // 4, factor_block, 0)
    wr1.wait_recv()
    fr1 = start(weight_send(4, left, 1, 1))
    wl0.wait_recv()
    fl0 = start(weight_send(5, right, 0, 3))

    for d in range(X):
        yu[d].wait_recv()
    lax.fori_loop(0, quarter // 32, choose_rows, 0)
    for copy in (wr0, wl1, fr1, fl0):
        copy.wait_recv()
    for d in (1, 2, 3):
        who = lax.rem(x + d, X)
        for s in range(TARGETS):
            for k in range(2):
                high, low = split(decoded(w_all, who, s, k))
                wall[who, s, k * R:(k + 1) * R, 0:R] = high
                wall[who, s, k * R:(k + 1) * R, R:2 * R] = low

    span = layers // 2
    for q in range(2):
        src = slice(q * span * qr, (q + 1) * span * qr)
        for xx in range(X):
            for s in range(TARGETS):
                got = dot(usel[xx, s, src, :], wall[xx, s])
                got = got[:, 0:R] + got[:, R:2 * R]
                for i in range(span):
                    t_part[i % 2, (q * span + i) // 2, xx * qr:(xx + 1) * qr, s * R:(s + 1) * R] = got[i * qr:(i + 1) * qr]
        for zz in range(q * nz // 2, (q + 1) * nz // 2):
            for s in range(TARGETS):
                coded(t_part[1 - c, zz, :, s * R:(s + 1) * R], t_out, zz, s)
            pair_copy(t_out, t_cx, tcx_s, tcx_r, zz).start()
    factored = [blocks // 4]

    def factor_more(count=1):
        upto = min(factored[0] + count, blocks)
        lax.fori_loop(factored[0], upto, factor_block, 0)
        factored[0] = upto

    factor_more(2)
    ring_reduce(t_part, t_out, t_cx, t_send, t_recv, tcx_s, tcx_r, trs_s, trs_r, t_own, lambda i: None, factor_more)

    def final_send(d):
        at = pl.ds(pl.multiple_of(lax.rem(x + d, X) * qr, qr), qr)
        return remote(t_own.at[at, :], t_fin.at[x], fin_s.at[d], fin_r.at[d], xdev(d))

    fins = [start(final_send(d)) for d in (2, 1, 3)]
    t_fin[x] = t_own[pl.ds(pl.multiple_of(x * qr, qr), qr), :]
    factor_more(blocks)
    for s in range(TARGETS):
        at = slice(s * R, (s + 1) * R)
        basis_ref[0, :, s, :] = dot(s_own[:, at], linv[s], 1, 1, precision=HIGH)
    for copy in fins:
        copy.wait_recv()
    for s in range(TARGETS):
        at = slice(s * R, (s + 1) * R)
        terms = jnp.concatenate([t_fin[i, :, at] for i in range(X)], axis=0)
        upd_ref[0, :, s, :] = dot(terms, linv[s], 1, 1, precision=HIGH) / tile

    for copy in pending:
        copy.wait_send()

    def pair_end(zz, carry):
        pair_copy(s_out, s_cx, scx_s, scx_r, zz).wait_send()
        pair_copy(t_out, t_cx, tcx_s, tcx_r, zz).wait_send()
        return carry

    lax.fori_loop(0, nz, pair_end, 0)


def on_device(panel_left, panel_right, test_matrix, ranks, offsets):
    rows, layers = lax.axis_size("row"), lax.axis_size("layer")
    tile = panel_left.shape[2]
    nz = layers // 2
    np_ = max(nz // 2, 1)
    br = tile // layers
    qr, hb, quarter = br // X, br // 2, tile // X
    dma = pltpu.SemaphoreType.DMA
    vmem = pltpu.VMEM
    I16 = jnp.int16
    ring = [
        vmem((2, nz, br, 2 * R), F32), vmem((nz, 2, br + EXTRA, R), I16), vmem((nz, 2, br + EXTRA, R), I16),
        vmem((4, np_, br + EXTRA, R), I16), vmem((4, np_, br + EXTRA, R), I16), vmem((br, 2 * R), F32),
    ]
    scratch = [
        vmem((1, 2, tile, R), BF), vmem((1, 2, tile, R), BF), vmem((tile, R), BF),
        pltpu.SMEM((1, 2), jnp.int32), pltpu.SMEM((1, TARGETS), jnp.int32), dma((5,)),
        vmem((2 * R, tile), BF), vmem((2, X * R, quarter), BF),
        vmem((2, tile, R), BF), vmem((X, 2, quarter, R), BF), vmem((X, 2, quarter, R), BF),
        vmem((2 * X, 2, quarter, R), BF), vmem((2 * X, 2, quarter, R), BF),
        vmem((X, TARGETS, quarter, 2 * R), BF),
        vmem((TARGETS, 8, R), F32), vmem((X, TARGETS, 8, R), F32),
        vmem((2, R + EXTRA, R), I16), vmem((FRONTS, 2, R + EXTRA, R), I16),
        vmem((X, TARGETS, 2, R, R), F32),
        *[vmem((TARGETS, 2, R + EXTRA, R), I16)] * 6,
        vmem((TARGETS, 2, R, R), F32),
        vmem((2, 2 * R, 2 * R), BF),
        *ring,
        vmem((2, nz, 2, br + EXTRA, R), I16), vmem((2, tile, 2 * R), BF),
        vmem((TARGETS, R, 2 * R), F32), vmem((TARGETS, R, R), F32), vmem((2 * R, 2 * R), F32),
        vmem((X, TARGETS, 2 * R, 2 * R), BF), vmem((X, TARGETS, 2, R + EXTRA, R), I16),
        *ring,
        vmem((X, qr, 2 * R), F32),
        dma((X, 2)), dma((X, 2)), dma((X,)), dma((X,)), dma((X, 2)), dma((X, 2)), dma((X,)), dma((X,)),
        dma((X,)), dma((X,)), dma((X,)), dma((X,)), dma((6, 2)), dma((6, 2)),
        dma((nz,)), dma((nz,)), dma((4, np_)), dma((4, np_)),
        dma((4, np_)), dma((4, np_)), dma((nz, 2)), dma((nz, 2)),
        dma((6,)), dma((6,)),
        dma((nz,)), dma((nz,)), dma((4, np_)), dma((4, np_)),
        dma((X,)), dma((X,)),
    ]
    inside = pl.BlockSpec(memory_space=pltpu.VMEM)
    outside = pl.BlockSpec(memory_space=pltpu.HBM)
    out = jax.ShapeDtypeStruct((1, br, TARGETS, R), F32)
    return pl.pallas_call(
        functools.partial(kernel, rows, layers, tile),
        out_shape=(out, out),
        in_specs=[outside] * 5,
        out_specs=(inside, inside),
        scratch_shapes=scratch,
        compiler_params=pltpu.CompilerParams(
            collective_id=0, has_side_effects=True, vmem_limit_bytes=64 * 2**20
        ),
        name="trailing_update",
    )(panel_left, panel_right, test_matrix, ranks, offsets)


def solution(mesh):
    return jax.shard_map(
        on_device,
        mesh=mesh,
        in_specs=(
            P("row", "layer", None, None),
            P("row", "layer", None, None),
            P(),
            P("row", "layer"),
            P("row", None),
        ),
        out_specs=(P("row", "layer", None, None), P("row", "layer", None, None)),
        check_vma=False,
    )
```

```python
import functools

import jax
import jax.numpy as jnp
from jax import lax
from jax.experimental import pallas as pl
from jax.experimental.pallas import tpu as pltpu
from jax.sharding import PartitionSpec as P

R = 128
X = 4
FRONTS = 4
TARGETS = 2
BF = jnp.bfloat16
F32 = jnp.float32
HIGH = lax.Precision.HIGHEST


def dot(a, b, ca=1, cb=0, precision=None):
    return lax.dot_general(
        a, b, (((ca,), (cb,)), ((), ())), precision=precision, preferred_element_type=F32
    )


def split(a):
    high = a.astype(BF)
    return high, (a - high.astype(F32)).astype(BF)


EXTRA = 16
STEPS = 128.0
TOP = 32766.0


def coded(value, ref, *at):
    n = value.shape[0]
    most = jnp.maximum(jnp.max(jnp.abs(value), axis=0, keepdims=True), 1e-30)
    code = jnp.ceil(jnp.log2(most) * STEPS) + 1.0
    ref[(*at, slice(0, n), slice(None))] = (
        jnp.round(value * (TOP * jnp.exp2(code * (-1.0 / STEPS)))).astype(jnp.int32).astype(jnp.int16)
    )
    ref[(*at, slice(n, n + EXTRA), slice(None))] = (
        jnp.broadcast_to(code, (EXTRA, value.shape[1])).astype(jnp.int32).astype(jnp.int16)
    )


def decoded(ref, *at):
    n = ref.shape[-2] - EXTRA
    code = ref[(*at, slice(n, n + EXTRA), slice(None))].astype(jnp.int32).astype(F32)[0:1]
    steps = ref[(*at, slice(0, n), slice(None))].astype(jnp.int32).astype(F32)
    return steps * (jnp.exp2(code * (1.0 / STEPS)) * (1.0 / TOP))


def kernel(
    rows, layers, tile,
    u_hbm, v_hbm, test_hbm, ranks_hbm, offs_hbm,
    basis_ref, upd_ref,
    u_ref, v_ref, test_ref, ranks_ref, offs_ref, in_sem, unt, vt, un, um, vm, vq, uq, usel, meta, metas, probe_own, probes, parts, far_out, plain_out, chain_in, plain_in, sum_out, sum_in, core,
    mix, s_part, s_out, s_cx, s_send, s_recv, s_own, s_all, s_full, gx, linv, reach, wall, w_all, t_part, t_out, t_cx, t_send, t_recv, t_own, t_fin,
    a2v_s, a2v_r, a2u_s, a2u_r, yv_s, yv_r, yu_s, yu_r, mt_s, mt_r, pr_s, pr_r, cr_s, cr_r,
    scx_s, scx_r, srs_s, srs_r, ag_s, ag_r, agc_s, agc_r, wg_s, wg_r, tcx_s, tcx_r, trs_s, trs_r, fin_s, fin_r,
):
    ny, nz = rows // X, layers // 2
    np_, nm = nz // 2, nz - 1 - nz // 2
    br = tile // layers
    qr, hb = br // X, br // 2
    quarter = tile // X
    row, layer = lax.axis_index("row"), lax.axis_index("layer")
    x, y = lax.rem(row, X), lax.div(row, X)
    z, c = lax.div(layer, 2), lax.rem(layer, 2)

    def xdev(d):
        return (y * X + lax.rem(x + d, X), layer)

    def ydev(d):
        return (lax.rem(y + d + ny, ny) * X + x, layer)

    def zdev(d):
        return (row, lax.rem(z + d + nz, nz) * 2 + c)

    mate = (row, z * 2 + 1 - c)
    loads = [
        pltpu.make_async_copy(src, dst, in_sem.at[i])
        for i, (src, dst) in enumerate((
            (ranks_hbm, ranks_ref), (offs_hbm, offs_ref), (v_hbm, v_ref), (u_hbm, u_ref), (test_hbm, test_ref)))
    ]
    for load in loads:
        load.start()
    barrier = pltpu.get_barrier_semaphore()

    def zcross(d):
        return (row, lax.rem(z + d + nz, nz) * 2 + 1 - c)

    friends = [
        xdev(1), xdev(2), xdev(3), ydev(1), ydev(-1), zdev(1), zdev(-1), zcross(1), zcross(-1), mate,
        zdev(2), zdev(-2), zcross(2), zcross(-2)]
    for friend in friends:
        pl.semaphore_signal(barrier, inc=1, device_id=friend, device_id_type=pl.DeviceIdType.MESH)

    def remote(src, dst, ssem, rsem, dev):
        return pltpu.make_async_remote_copy(
            src_ref=src, dst_ref=dst, send_sem=ssem, recv_sem=rsem,
            device_id=dev, device_id_type=pl.DeviceIdType.MESH,
        )

    pending = []

    def start(copy):
        copy.start()
        pending.append(copy)
        return copy

    loads[0].wait()
    loads[1].wait()
    lanes = lax.broadcasted_iota(jnp.int32, (1, R), 1)
    live = [(lanes < ranks_ref[0, k]).astype(F32).astype(BF) for k in range(2)]

    def mask_quarter(d):
        xx = lax.rem(x + d, X)

        def body(i, carry):
            src = pl.ds(pl.multiple_of(i * br + xx * qr, qr), qr)
            dst = pl.ds(pl.multiple_of(i * qr, qr), qr)
            for k in range(2):
                v = v_ref[0, k, src, :] * live[k]
                if d == 0:
                    vq[X + x, k, dst, :] = v
                else:
                    vm[xx, k, dst, :] = v
            return carry

        lax.fori_loop(0, layers, body, 0)

    def slot_of(d):
        return lax.rem(x - d + X, X)

    def a2a(d, src, dst, ss, rs):
        return remote(src.at[lax.rem(x + d, X)], dst.at[X + x], ss.at[d], rs.at[d], xdev(d))

    def ysend(d, buf, ss, rs):
        return remote(buf.at[X + slot_of(d)], buf.at[slot_of(d)], ss.at[d], rs.at[d], ydev(1))

    yv = {
        (d, k): remote(
            vq.at[X + slot_of(d), k], vq.at[slot_of(d), k], yv_s.at[d, k], yv_r.at[d, k], ydev(1))
        for d in range(X) for k in range(2)
    }
    av = {
        (d, k): remote(
            vm.at[lax.rem(x + d, X), k], vq.at[X + x, k], a2v_s.at[d, k], a2v_r.at[d, k], xdev(d))
        for d in (1, 2, 3) for k in range(2)
    }
    loads[2].wait()
    mask_quarter(0)
    pl.semaphore_wait(barrier, len(friends))
    start(yv[0, 0])
    start(yv[0, 1])
    mask_quarter(1)
    start(av[1, 0])
    mask_quarter(3)
    start(av[3, 0])
    start(av[1, 1])
    start(av[3, 1])
    mask_quarter(2)
    for s in range(TARGETS):
        meta[s, :, :] = jnp.full((8, R), offs_ref[0, s], jnp.int32).astype(F32)
    metas[x] = meta[...]
    mts = {d: start(remote(meta, metas.at[x], mt_s.at[d], mt_r.at[d], xdev(d))) for d in (1, 2, 3)}
    loads[3].wait()
    loads[4].wait()

    def mask_left(i, carry):
        src = pl.ds(pl.multiple_of(i * br, br), br)
        for k in range(2):
            u = u_ref[0, k, src, :] * live[k]
            un[k, src, :] = u
            unt[k * R:(k + 1) * R, src] = u.T
            for xx in range(X):
                um[xx, k, pl.ds(pl.multiple_of(i * qr, qr), qr), :] = u[xx * qr:(xx + 1) * qr]
        return carry

    lax.fori_loop(0, layers, mask_left, 0)
    uq[X + x] = um[x]
    probed = dot(unt[...], test_ref[...])
    for k in range(2):
        coded(probed[k * R:(k + 1) * R], probe_own, k)
    pry = start(remote(probe_own, probes.at[FRONTS - 1], pr_s.at[0], pr_r.at[0], ydev(1)))
    for d in (1, 3):
        av[d, 0].wait_recv()
        start(yv[d, 0])
    start(av[2, 0])

    def probe_send(d, src):
        return remote(src, probes.at[d - 1], pr_s.at[d], pr_r.at[d], xdev(d))

    for d in (1, 2, 3):
        @pl.when(x + d < X)
        def _(d=d):
            probe_send(d, probe_own).start()
    def turn(d, k):
        j = slot_of(d)
        vt[k, pl.ds(pl.multiple_of(j * R, R), R), :] = vq[X + j, k].T

    turn(0, 0)
    turn(0, 1)
    turn(1, 0)
    turn(3, 0)
    av[2, 0].wait_recv()
    start(yv[2, 0])
    start(av[2, 1])
    turn(2, 0)
    pry.wait_recv()
    for d in (1, 2, 3):
        @pl.when(x + d >= X)
        def _(d=d):
            probe_send(d, probes.at[FRONTS - 1]).start()
    prx = [probe_send(d, probe_own) for d in (1, 2, 3)]
    pending.extend(prx)
    au = {d: a2a(d, um, uq, a2u_s, a2u_r) for d in (1, 2, 3)}
    for copy in mts.values():
        copy.wait_recv()

    marks = [[metas[xx, s, 0:1, :] for s in range(TARGETS)] for xx in range(X)]
    parts[...] = jnp.zeros_like(parts)

    def add_cores(k, slot, first, back):
        found = dot(vt[k, first * R:, :], vq[slot, k])
        for xx in range(first, X):
            block = found[(xx - first) * R:(xx - first + 1) * R]
            for s in range(TARGETS):
                parts[xx, s, k] += block * (marks[xx][s] == back(xx)).astype(F32)

    def add_same(k):
        for j in range(X - 1):
            add_cores(k, X + j, j + 1, lambda xx: float(xx - j))

    def add_arrived(d, k):
        yv[d, k].wait_recv()
        j = slot_of(d)
        add_cores(k, j, 0, lambda xx: (X + xx - j).astype(F32))

    far = lax.rem(x + 2, X)
    right, left = lax.rem(x + 1, X), lax.rem(x + 3, X)

    def core_hop(i, k, out, into, s, d):
        return remote(out.at[s, k], into.at[s, k], cr_s.at[i, k], cr_r.at[i, k], xdev(d))

    trips = [(far, far_out, chain_in, s, 2) for s in range(2)]
    trips += [(right, plain_out, plain_in, s, 1) for s in range(2)] + [(left, sum_out, sum_in, s, 3) for s in range(2)]

    def cores_out(k):
        for i, (who, out, into, s, d) in enumerate(trips):
            coded(parts[who, s, k], out, s, k)
            start(core_hop(i, k, out, into, s, d))

    def cores_in(k):
        for i, (who, out, into, s, d) in enumerate(trips):
            core_hop(i, k, out, into, s, d).wait_recv()
        for s in range(TARGETS):
            core[s, k] = (
                parts[x, s, k] + decoded(chain_in, s, k) + decoded(plain_in, s, k) + decoded(sum_in, s, k))

    def mix_layer(k):
        for s in range(TARGETS):
            back = jnp.clip(offs_ref[0, s] - 1, 0, FRONTS - 1)
            mixed = dot(core[s, k], decoded(probes, back, k), precision=HIGH)
            high, low = split(mixed)
            mix[0, k * R:(k + 1) * R, s * R:(s + 1) * R] = high
            mix[1, k * R:(k + 1) * R, s * R:(s + 1) * R] = low

    yu = [ysend(d, uq, yu_s, yu_r) for d in range(X)]
    add_same(0)
    for d in (0, 1, 3):
        add_arrived(d, 0)
    av[1, 1].wait_recv()
    start(yv[1, 1])
    av[3, 1].wait_recv()
    turn(1, 1)
    turn(3, 1)
    yv[2, 0].wait_recv()
    start(yv[3, 1])
    av[2, 1].wait_recv()
    start(yv[2, 1])
    last = slot_of(2)
    add_cores(0, last, 0, lambda xx: (X + xx - last).astype(F32))
    cores_out(0)
    turn(2, 1)
    add_same(1)
    start(au[1])
    start(au[3])
    add_arrived(0, 1)
    add_arrived(1, 1)
    for copy in prx:
        copy.wait_recv()
    cores_in(0)
    mix_layer(0)
    add_arrived(3, 1)
    yv[2, 1].wait_recv()
    start(yu[0])
    add_cores(1, last, 0, lambda xx: (X + xx - last).astype(F32))
    cores_out(1)
    cores_in(1)

    start(au[2])
    mix_layer(1)

    def order(i):
        half = lax.div(i + 1, 2)
        off = jnp.where(lax.rem(i, 2) == 1, half - np_, np_ - half)
        return lax.rem(z + off + nz, nz)

    def pair_copy(out, cx, ss, rs, zz):
        return remote(out.at[zz], cx.at[zz], ss.at[zz], rs.at[zz], mate)

    def sketch_rows(i, carry):
        zz = order(i)
        src = pl.ds(pl.multiple_of(zz * 2 * br, 2 * br), 2 * br)
        both = jnp.concatenate([un[0, src, :], un[1, src, :]], axis=1)
        got = dot(both, mix[0]) + dot(both, mix[1])
        s_part[0, zz] = got[:br]
        s_part[1, zz] = got[br:]
        for s in range(TARGETS):
            coded(s_part[1 - c, zz, :, s * R:(s + 1) * R], s_out, zz, s)
        pair_copy(s_out, s_cx, scx_s, scx_r, zz).start()
        return carry

    chains = [(1, 0, np_), (-1, 0, nm), (1, 1, nm), (-1, 1, np_)]
    groups = ((0, 3), (1, 2))

    def ring_reduce(part, out, cx, send, recv, ss_cx, rs_cx, ss, rs, own, before, between):
        waited = set()

        def term(off, h):
            zz = lax.rem(z + off + 2 * nz, nz)
            if off % nz not in waited:
                waited.add(off % nz)
                pair_copy(out, cx, ss_cx, rs_cx, zz).wait_recv()
            return part[c, zz, :, h * R:(h + 1) * R] + decoded(cx, zz, h)

        def hop(ch, i):
            return remote(send.at[ch, i], recv.at[ch, i], ss.at[ch, i], rs.at[ch, i], zdev(chains[ch][0]))

        before(0)
        for i in range(np_):
            for group in groups:
                if i == 0 and group is groups[1] and np_ > 1:
                    before(1)
                for ch in group:
                    sgn, h, n = chains[ch]
                    if i >= n:
                        continue
                    value = term(sgn * (n - i), h)
                    if i > 0:
                        hop(ch, i - 1).wait_recv()
                        value = value + decoded(recv, ch, i - 1)
                    coded(value, send, ch, i)
                    start(hop(ch, i))
                between()
            if i + 2 < np_:
                before(i + 2)
        for h in range(2):
            value = term(0, h)
            for ch, (sgn, hh, n) in enumerate(chains):
                if hh == h and n > 0:
                    hop(ch, n - 1).wait_recv()
                    value = value + decoded(recv, ch, n - 1)
            own[:, h * R:(h + 1) * R] = value

    def sketch_more(i):
        lax.fori_loop(max(2 * i - 1, 0), nz if i == np_ - 1 else 2 * i + 1, sketch_rows, 0)
        if i == min(1, np_ - 1):
            for d in (1, 3):
                au[d].wait_recv()
                start(yu[d])

    ring_reduce(
        s_part, s_out, s_cx, s_send, s_recv, scx_s, scx_r, srs_s, srs_r, s_own, sketch_more, lambda: None)
    au[2].wait_recv()
    start(yu[2])

    for h in range(2):
        coded(s_own[:, h * R:(h + 1) * R], s_all, c, z, h)

    def gather_leg(ch, i):
        sgn = chains[ch][0]
        return (0, sgn * (i + 1)) if i < 2 else (-2 * sgn, sgn * (i - 1))

    def gather_hop(ch, i):
        h = chains[ch][1]
        off, d = gather_leg(ch, i)
        zz = lax.rem(z + off + nz, nz)
        return remote(s_all.at[c, zz, h], s_all.at[c, zz, h], ag_s.at[ch, i], ag_r.at[ch, i], zdev(d))

    def to_mate(off, h):
        zz = lax.rem(z + off + nz, nz)
        at = (off + nz) % nz
        return remote(s_all.at[c, zz, h], s_all.at[c, zz, h], agc_s.at[at, h], agc_r.at[at, h], mate)

    def spread(par, off, h):
        zz = lax.rem(z + off + nz, nz)
        high, low = split(decoded(s_all, par, zz, h))
        to = pl.ds(pl.multiple_of((zz * 2 + par) * br, br), br)
        s_full[0, to, h * R:(h + 1) * R] = high
        s_full[1, to, h * R:(h + 1) * R] = low

    def launch(ch, i):
        sgn, h, n = chains[ch]
        start(gather_hop(ch, i))
        if n == np_ and i == n - 1:
            off, d = gather_leg(ch, i)
            zz = lax.rem(z + off + nz, nz)
            at = (-sgn * n) % nz
            start(remote(s_all.at[c, zz, h], s_all.at[c, zz, h], agc_s.at[at, h], agc_r.at[at, h], zcross(d)))

    def use(off):
        zz = lax.rem(z + off + nz, nz)
        src = pl.ds(pl.multiple_of(zz * 2 * br, 2 * br), 2 * br)
        reach[...] += dot(unt[:, src], s_full[0, src, :]) + dot(unt[:, src], s_full[1, src, :])
        for s in range(TARGETS):
            at = slice(s * R, (s + 1) * R)
            high, low = s_full[0, src, at], s_full[1, src, at]
            gx[s] += dot(high, jnp.concatenate([high, low], axis=1), 0, 0)

    for ch in groups[0]:
        for i in range(min(2, chains[ch][2])):
            launch(ch, i)
    reach[...] = jnp.zeros_like(reach)
    gx[...] = jnp.zeros_like(gx)
    for h in range(2):
        spread(c, 0, h)
    for ch in groups[1]:
        for i in range(min(2, chains[ch][2])):
            launch(ch, i)
    for h in range(2):
        start(to_mate(0, h))
    late = [(0, h) for h in range(2)]
    for i in range(np_):
        got = []
        ready = sorted({i, -i})
        for group in groups:
            for ch in group:
                sgn, h, n = chains[ch]
                if i < n:
                    gather_hop(ch, i).wait_recv()
                    for j in range(2, n if i == 1 else 2):
                        launch(ch, j)
                    off = -sgn * (i + 1)
                    if i < np_ - 1:
                        start(to_mate(off, h))
                    got.append((off, h))
            if group is groups[0]:
                for off, h in late:
                    to_mate(off, h).wait_recv()
                    spread(1 - c, off, h)
                use(ready[0])
            else:
                for off, h in got:
                    spread(c, off, h)
                for off in ready[1:]:
                    use(off)
        late = got
    for off, h in late:
        to_mate(off, h).wait_recv()
        spread(1 - c, off, h)
    use(np_)

    pick16 = [[[(marks[xx][s] == o).astype(F32).astype(BF) for o in range(1, FRONTS + 1)]
               for s in range(TARGETS)] for xx in range(X)]

    def choose_rows(i, carry):
        src = pl.ds(pl.multiple_of(i * 32, 32), 32)
        for xx in range(X):
            for k in range(2):
                cand = [uq[X + xx - o, k, src, :] for o in range(1, FRONTS + 1)]
                for s in range(TARGETS):
                    total = cand[0] * pick16[xx][s][0]
                    for o in range(1, FRONTS):
                        total = total + cand[o] * pick16[xx][s][o]
                    usel[xx, s, src, k * R:(k + 1) * R] = total
        return carry

    for s in range(TARGETS):
        for k in range(2):
            weight = dot(core[s, k], reach[k * R:(k + 1) * R, s * R:(s + 1) * R], 0, 0, precision=HIGH)
            coded(weight, w_all, x, s, k)
            high, low = split(weight)
            wall[x, s, k * R:(k + 1) * R, 0:R] = high
            wall[x, s, k * R:(k + 1) * R, R:2 * R] = low

    def weight_send(i, who, s, d):
        return remote(w_all.at[who, s], w_all.at[who, s], wg_s.at[i], wg_r.at[i], xdev(d))

    shares = [start(weight_send(i, x, i % 2, d)) for i, d in enumerate((2, 2, 1, 1, 3, 3))]

    eye = (lax.broadcasted_iota(jnp.int32, (R, R), 0) == lax.broadcasted_iota(jnp.int32, (R, R), 1)).astype(F32)
    for s in range(TARGETS):
        cross = gx[s, :, R:2 * R]
        gx[s, :, 0:R] = (gx[s, :, 0:R] + (cross + cross.T)) / tile
        gx[s, :, R:2 * R] = eye

    lane8 = lax.broadcasted_iota(jnp.int32, (8, R), 1)
    sub8 = lax.broadcasted_iota(jnp.int32, (8, R), 0)

    def factor_block(b, carry):
        r0 = pl.multiple_of(b * 8, 8)
        for s in range(TARGETS):
            gg = gx[s, pl.ds(r0, 8), 0:R]
            xx = gx[s, pl.ds(r0, 8), R:2 * R]
            cols = [
                jnp.broadcast_to(
                    jnp.sum(jnp.where(lane8 == r0 + j, gg, 0.0), axis=1, keepdims=True), (8, R))
                for j in range(8)
            ]
            diag = jnp.ones((8, R), F32)
            for j in range(8):
                pivot = cols[j][j:j + 1]
                diag = jnp.where(sub8 == j, pivot, diag)
                f = jnp.where(sub8 > j, cols[j] / pivot, 0.0)
                for m in range(j + 1, 8):
                    cols[m] = cols[m] - f * cols[m][j:j + 1]
                gg = gg - f * gg[j:j + 1]
                xx = xx - f * xx[j:j + 1]
            linv[s, pl.ds(r0, 8), :] = xx / jnp.sqrt(diag)
            lead = jnp.where(lane8 >= r0 + 8, gg / diag, 0.0)
            gx[s] -= dot(lead, jnp.concatenate([gg, xx], axis=1), 0, 0, precision=HIGH)
        return carry

    blocks = R // 8
    lax.fori_loop(0, blocks // 4, factor_block, 0)

    for d in range(X):
        yu[d].wait_recv()
    lax.fori_loop(0, quarter // 32, choose_rows, 0)
    for copy in shares:
        copy.wait_recv()
    for d in (1, 2, 3):
        who = lax.rem(x + d, X)
        for s in range(TARGETS):
            for k in range(2):
                high, low = split(decoded(w_all, who, s, k))
                wall[who, s, k * R:(k + 1) * R, 0:R] = high
                wall[who, s, k * R:(k + 1) * R, R:2 * R] = low

    span = layers // 2
    for q in range(2):
        src = slice(q * span * qr, (q + 1) * span * qr)
        for xx in range(X):
            for s in range(TARGETS):
                got = dot(usel[xx, s, src, :], wall[xx, s])
                got = got[:, 0:R] + got[:, R:2 * R]
                for i in range(span):
                    t_part[i % 2, (q * span + i) // 2, xx * qr:(xx + 1) * qr, s * R:(s + 1) * R] = got[i * qr:(i + 1) * qr]
        for zz in range(q * nz // 2, (q + 1) * nz // 2):
            for s in range(TARGETS):
                coded(t_part[1 - c, zz, :, s * R:(s + 1) * R], t_out, zz, s)
            pair_copy(t_out, t_cx, tcx_s, tcx_r, zz).start()
    factored = [blocks // 4]

    def factor_more(count=1):
        upto = min(factored[0] + count, blocks)
        lax.fori_loop(factored[0], upto, factor_block, 0)
        factored[0] = upto

    factor_more(2)
    ring_reduce(t_part, t_out, t_cx, t_send, t_recv, tcx_s, tcx_r, trs_s, trs_r, t_own, lambda i: None, factor_more)

    def final_send(d):
        at = pl.ds(pl.multiple_of(lax.rem(x + d, X) * qr, qr), qr)
        return remote(t_own.at[at, :], t_fin.at[x], fin_s.at[d], fin_r.at[d], xdev(d))

    fins = [start(final_send(d)) for d in (2, 1, 3)]
    t_fin[x] = t_own[pl.ds(pl.multiple_of(x * qr, qr), qr), :]
    factor_more(blocks)
    for s in range(TARGETS):
        at = slice(s * R, (s + 1) * R)
        basis_ref[0, :, s, :] = dot(s_own[:, at], linv[s], 1, 1, precision=HIGH)
    for copy in fins:
        copy.wait_recv()
    for s in range(TARGETS):
        at = slice(s * R, (s + 1) * R)
        terms = jnp.concatenate([t_fin[i, :, at] for i in range(X)], axis=0)
        upd_ref[0, :, s, :] = dot(terms, linv[s], 1, 1, precision=HIGH) / tile

    for copy in pending:
        copy.wait_send()

    def pair_end(zz, carry):
        pair_copy(s_out, s_cx, scx_s, scx_r, zz).wait_send()
        pair_copy(t_out, t_cx, tcx_s, tcx_r, zz).wait_send()
        return carry

    lax.fori_loop(0, nz, pair_end, 0)


def on_device(panel_left, panel_right, test_matrix, ranks, offsets):
    rows, layers = lax.axis_size("row"), lax.axis_size("layer")
    tile = panel_left.shape[2]
    nz = layers // 2
    np_ = max(nz // 2, 1)
    br = tile // layers
    qr, hb, quarter = br // X, br // 2, tile // X
    dma = pltpu.SemaphoreType.DMA
    vmem = pltpu.VMEM
    I16 = jnp.int16
    ring = [
        vmem((2, nz, br, 2 * R), F32), vmem((nz, 2, br + EXTRA, R), I16), vmem((nz, 2, br + EXTRA, R), I16),
        vmem((4, np_, br + EXTRA, R), I16), vmem((4, np_, br + EXTRA, R), I16), vmem((br, 2 * R), F32),
    ]
    scratch = [
        vmem((1, 2, tile, R), BF), vmem((1, 2, tile, R), BF), vmem((tile, R), BF),
        pltpu.SMEM((1, 2), jnp.int32), pltpu.SMEM((1, TARGETS), jnp.int32), dma((5,)),
        vmem((2 * R, tile), BF), vmem((2, X * R, quarter), BF),
        vmem((2, tile, R), BF), vmem((X, 2, quarter, R), BF), vmem((X, 2, quarter, R), BF),
        vmem((2 * X, 2, quarter, R), BF), vmem((2 * X, 2, quarter, R), BF),
        vmem((X, TARGETS, quarter, 2 * R), BF),
        vmem((TARGETS, 8, R), F32), vmem((X, TARGETS, 8, R), F32),
        vmem((2, R + EXTRA, R), I16), vmem((FRONTS, 2, R + EXTRA, R), I16),
        vmem((X, TARGETS, 2, R, R), F32),
        *[vmem((TARGETS, 2, R + EXTRA, R), I16)] * 6,
        vmem((TARGETS, 2, R, R), F32),
        vmem((2, 2 * R, 2 * R), BF),
        *ring,
        vmem((2, nz, 2, br + EXTRA, R), I16), vmem((2, tile, 2 * R), BF),
        vmem((TARGETS, R, 2 * R), F32), vmem((TARGETS, R, R), F32), vmem((2 * R, 2 * R), F32),
        vmem((X, TARGETS, 2 * R, 2 * R), BF), vmem((X, TARGETS, 2, R + EXTRA, R), I16),
        *ring,
        vmem((X, qr, 2 * R), F32),
        dma((X, 2)), dma((X, 2)), dma((X,)), dma((X,)), dma((X, 2)), dma((X, 2)), dma((X,)), dma((X,)),
        dma((X,)), dma((X,)), dma((X,)), dma((X,)), dma((6, 2)), dma((6, 2)),
        dma((nz,)), dma((nz,)), dma((4, np_)), dma((4, np_)),
        dma((4, np_)), dma((4, np_)), dma((nz, 2)), dma((nz, 2)),
        dma((6,)), dma((6,)),
        dma((nz,)), dma((nz,)), dma((4, np_)), dma((4, np_)),
        dma((X,)), dma((X,)),
    ]
    inside = pl.BlockSpec(memory_space=pltpu.VMEM)
    outside = pl.BlockSpec(memory_space=pltpu.HBM)
    out = jax.ShapeDtypeStruct((1, br, TARGETS, R), F32)
    return pl.pallas_call(
        functools.partial(kernel, rows, layers, tile),
        out_shape=(out, out),
        in_specs=[outside] * 5,
        out_specs=(inside, inside),
        scratch_shapes=scratch,
        compiler_params=pltpu.CompilerParams(
            collective_id=0, has_side_effects=True, vmem_limit_bytes=64 * 2**20
        ),
        name="trailing_update",
    )(panel_left, panel_right, test_matrix, ranks, offsets)


def solution(mesh):
    return jax.shard_map(
        on_device,
        mesh=mesh,
        in_specs=(
            P("row", "layer", None, None),
            P("row", "layer", None, None),
            P(),
            P("row", "layer"),
            P("row", None),
        ),
        out_specs=(P("row", "layer", None, None), P("row", "layer", None, None)),
        check_vma=False,
    )
```
